32 devices in a mesh: group: 2 (over x), space: 16 (over z, y, core).
Axes of the slice: x: 2, y: 2, z: 4, core: 2. Of those that a mesh axis runs over, the one named last changes fastest.
Arguments:
- snapshots: bfloat16 [32, 3, 256, 128], P('group', None, 'space'), parts along dimension 0, may hold values from -8 to 8
- basis: bfloat16 [128, 3, 128, 256], P('group', None, 'space'), parts along dimension 0, may hold values from -6 to 6
- mode_weights: float32 [128], P('group'), parts along dimension 0, may hold values from 0.5 to 4
- land_mask: int32 [256, 128], P('space'), may hold values 0 or 1
- scale_index: int32 [128], replicated, may hold values from 0 to 15
- scale_values: float32 [16], replicated, may hold values from 0.06 to 0.24
Outputs:
- new_basis: bfloat16 [128, 3, 128, 256], P('group', None, 'space'), parts along dimension 0
- coefficients: float32 [32, 64], P('group'), parts along dimension 0
The draws below stay inside these ranges and needn't reach their ends.
There are 2 independent parts, one for each index of `group`. The reference program is written for one: setup_inputs(seed, part) draws one part's arguments, and reference() takes and returns one part's arrays. A program takes and returns all parts, laid end to end along the dimension named above; an argument that names none is the same for every part. Nothing has to cross between parts.
Inputs may be any that keep to these rules, and one draw needn't show every extreme that they name: `land_mask`: 1 marks ocean, 0 land. Row y uses scale_values[scale_index[y]].
All inputs are finite; a program needn't handle non-finite values. No bound on the sum of `land_mask` on one device may be relied on, other than what follows from the above.
Results may differ from the reference program's by a relative error of at most 0.0057.
Values may be sent and summed in bfloat16 or wider, within the bound.
A program may use at most 128 MiB of HBM per device.

```python
import math
import jax
import jax.numpy as jnp
from jax import lax

SNAPS = 16
FIELDS = 3
MODES = 64
NSCALE = 16
NX = 256
NY = 128


def touch_ends(values, own_key, low, top_value):
    place = [jax.random.randint(jax.random.fold_in(own_key, axis), (), 0, length) for axis, length in enumerate(values.shape)]
    longest = values.shape.index(max(values.shape))
    beside = place[:longest] + [(place[longest] + 1) % values.shape[longest]] + place[longest + 1:]
    return values.at[tuple(place)].set(low).at[tuple(beside)].set(top_value)


def block_levels(own_key, dims, shards, smallest, high):
    def one(dim, blocks):
        draws = jax.random.uniform(jax.random.fold_in(jax.random.fold_in(own_key, 6), dim), (blocks,), jnp.float32, smallest / len(shards), high / len(shards))
        return jnp.repeat(jnp.exp(draws), dims[dim] // blocks).reshape((-1,) + (1,) * (len(dims) - dim - 1))

    factor_of = one(*shards[0])
    for cut in shards[1:]:
        factor_of = factor_of * one(*cut)
    return factor_of


def bell_draw(rng, extent, spread, most, split=(), held_as=jnp.bfloat16):
    array = spread * jax.random.normal(rng, extent, jnp.float32)
    if split:
        array = array * block_levels(rng, extent, split, -0.22, 0.18)
    return jnp.clip(array, -most, most).astype(held_as)


def setup_inputs(seed: int = 0, part: int = 0) -> dict:
    seeds = jax.random.split(jax.random.key(seed), 7)
    own_keys = jax.random.split(jax.random.fold_in(seeds[6], part), 7)
    return {
        "snapshots": bell_draw(own_keys[0], (SNAPS, FIELDS, NX, NY), 2.0, 8.0, ((2, 16),)),
        "basis": bell_draw(own_keys[1], (MODES, FIELDS, NY, NX), 1.0, 6.0, ((2, 16),)),
        "mode_weights": jnp.clip(jnp.exp(jax.random.uniform(own_keys[2], (MODES,), jnp.float32, math.log(0.5), math.log(4.0))), 0.5, 4.0),
        "land_mask": touch_ends((jax.random.randint(seeds[3], (NX, NY), 0, 5) < 4).astype(jnp.int32), jax.random.fold_in(seeds[3], 1), 0, 1),
        "scale_index": touch_ends(jax.random.randint(seeds[4], (NY,), 0, NSCALE), jax.random.fold_in(seeds[4], 1), 0, NSCALE - 1).astype(jnp.int32),
        "scale_values": jnp.clip(jnp.exp(jax.random.uniform(seeds[5], (NSCALE,), jnp.float32, math.log(0.06), math.log(0.24))), 0.06, 0.24),
    }


PASS_COEFS = (1.0, 0.95, 0.85, 0.7, 0.5, 0.3)

def latitude_scale(scale_index, scale_values):
    levels = jnp.arange(scale_values.shape[0], dtype=jnp.int32)
    matches = (scale_index[None, :] == levels[:, None]).astype(jnp.float32)
    return lax.optimization_barrier(jnp.sum(matches * scale_values[:, None], axis=0))

def reference(snapshots, basis, mode_weights, land_mask, scale_index, scale_values):
    lat_scale = latitude_scale(scale_index, scale_values)
    ocean = land_mask.astype(jnp.float32)
    east_mask = jnp.roll(ocean, -1, 0)
    west_mask = jnp.roll(ocean, 1, 0)
    north_mask = jnp.pad(ocean, ((0, 0), (0, 1)))[:, 1:]
    south_mask = jnp.pad(ocean, ((0, 0), (1, 0)))[:, :-1]
    fields_now = snapshots.astype(jnp.float32)
    for pass_coef in PASS_COEFS:
        factor = pass_coef * lat_scale
        east_flux = east_mask * (jnp.roll(fields_now, -1, 2) - fields_now)
        west_flux = west_mask * (jnp.roll(fields_now, 1, 2) - fields_now)
        padded = jnp.pad(fields_now, ((0, 0), (0, 0), (0, 0), (1, 1)))
        north_flux = north_mask * (padded[..., 2:] - fields_now)
        south_flux = south_mask * (padded[..., :-2] - fields_now)
        fields_now = fields_now + factor * (ocean * (east_flux + west_flux + north_flux + south_flux))
    filtered = (ocean * fields_now).astype(jnp.bfloat16)
    total_cells = float(FIELDS * NX * NY)
    high = lax.Precision.HIGHEST
    cross_sum = jnp.einsum('sfxy,kfyx->sk', filtered.astype(jnp.float32), basis.astype(jnp.float32), precision=high)
    coefficients = cross_sum / math.sqrt(total_cells)
    coeff_b = coefficients.astype(jnp.bfloat16)
    update = mode_weights[:, None, None, None] * basis.astype(jnp.float32) + jnp.einsum('sk,sfxy->kfyx', coeff_b.astype(jnp.float32), filtered.astype(jnp.float32), precision=high)
    update_rows = update.reshape(update.shape[0], -1)
    gram_matrix = jnp.dot(update_rows, update_rows.T, precision=high) / total_cells
    chol_factor = jnp.linalg.cholesky(gram_matrix)
    solved = jax.scipy.linalg.solve_triangular(chol_factor, update_rows, lower=True)
    new_basis = solved.reshape(basis.shape).astype(jnp.bfloat16)
    return (new_basis, coefficients)
```

```python
import functools
import math

import jax
import jax.numpy as jnp
from jax import lax
from jax.experimental import pallas as pl
from jax.experimental.pallas import tpu as pltpu
from jax.sharding import PartitionSpec as P

PASS_COEFS = (1.0, 0.95, 0.85, 0.7, 0.5, 0.3)
HALO = len(PASS_COEFS)
LANES = 128
HIGH = lax.Precision.HIGHEST
MESH = pl.DeviceIdType.MESH
VMEM = pl.BlockSpec(memory_space=pltpu.VMEM)


def peer(step, n):
    return lax.rem(lax.axis_index("space") + step, n)


def greet(n):
    group = lax.axis_index("group")
    barrier = pltpu.get_barrier_semaphore()

    def signal(step, carry):
        pl.semaphore_signal(barrier, inc=1, device_id=(group, peer(step, n)), device_id_type=MESH)
        return carry

    lax.fori_loop(1, n, signal, 0)
    pl.semaphore_wait(barrier, n - 1)


def exchange(n, make_copy):
    def start(step, carry):
        make_copy(peer(step, n), lax.axis_index("space")).start()
        return carry

    def wait_recv(step, carry):
        source = peer(n - step, n)
        make_copy(source, source).wait_recv()
        return carry

    def wait_send(step, carry):
        make_copy(peer(step, n), lax.axis_index("space")).wait_send()
        return carry

    lax.fori_loop(1, n, start, 0)
    return lambda: lax.fori_loop(1, n, wait_recv, 0), lambda: lax.fori_loop(1, n, wait_send, 0)


def spread_kernel(n, cols, send_ref, recv_ref, land, send_sem, recv_sem):
    me = lax.axis_index("space")
    group = lax.axis_index("group")
    greet(n)

    def make_copy(dst, slot):
        return pltpu.make_async_remote_copy(
            src_ref=send_ref.at[:, :, pl.ds(pl.multiple_of(dst * LANES, LANES), LANES)],
            dst_ref=land.at[:, pl.ds(pl.multiple_of(slot * cols, cols), cols), :],
            send_sem=send_sem.at[dst],
            recv_sem=recv_sem.at[slot],
            device_id=(group, dst),
            device_id_type=MESH,
        )

    arrived, sent = exchange(n, make_copy)
    land[:, pl.ds(pl.multiple_of(me * cols, cols), cols), :] = send_ref[
        :, :, pl.ds(pl.multiple_of(me * LANES, LANES), LANES)
    ]
    arrived()
    recv_ref[...] = land[...]
    sent()


def sum_kernel(n, part_ref, total_ref, land, send_sem, recv_sem):
    me = lax.axis_index("space")
    group = lax.axis_index("group")
    greet(n)

    def make_copy(dst, slot):
        return pltpu.make_async_remote_copy(
            src_ref=part_ref,
            dst_ref=land.at[slot],
            send_sem=send_sem.at[dst],
            recv_sem=recv_sem.at[slot],
            device_id=(group, dst),
            device_id_type=MESH,
        )

    arrived, sent = exchange(n, make_copy)
    land[me] = part_ref[...]
    arrived()
    total = land[0]
    for slot in range(1, n):
        total = total + land[slot]
    total_ref[...] = total
    sent()


def filter_kernel(win, groups, recv_ref, basis_ref, index_ref, values_ref, rows_ref, gram_ref, stack, weight):
    tiles = recv_ref.shape[0] - 1
    nx = recv_ref.shape[1]
    own = win - 2 * HALO
    ny = index_ref.shape[1]
    modes_rows = basis_ref.shape[0]
    total_rows, fy_count = rows_ref.shape[0], rows_ref.shape[1] // nx
    me = lax.axis_index("space")

    for c in range(nx // LANES):
        stack[c, 0:modes_rows, :] = basis_ref[:, c * LANES : (c + 1) * LANES].astype(jnp.float32)

    lat = jnp.zeros((1, ny), jnp.float32)
    for level in range(values_ref.shape[1]):
        lat = lat + jnp.where(index_ref[...] == level, values_ref[0:1, level : level + 1], 0.0)
    lane = lax.broadcasted_iota(jnp.int32, (ny, LANES), 1)
    row = lax.broadcasted_iota(jnp.int32, (ny, LANES), 0)
    pick = jnp.zeros((ny, LANES), jnp.float32)
    for g in range(groups):
        here = (lane >= g * win) & (lane < (g + 1) * win)
        pick = jnp.where(here & (row == me * own - HALO + lane - g * win), 1.0, pick)
    lat_lane = jnp.dot(jnp.broadcast_to(lat, (8, ny)), pick, precision=HIGH, preferred_element_type=jnp.float32)[0:1]

    def east(a):
        return pltpu.roll(a, nx - 1, 0)

    def west(a):
        return pltpu.roll(a, 1, 0)

    def north(a):
        return pltpu.roll(a, LANES - 1, 1)

    def south(a):
        return pltpu.roll(a, 1, 1)

    ocean = recv_ref[tiles].astype(jnp.float32)
    base = ocean * lat_lane
    sides = (east, west, north, south)
    for i, side in enumerate(sides):
        weight[i] = base * side(ocean)
    weight[4] = ocean

    @pl.loop(0, tiles)
    def _(t):
        f = recv_ref[t].astype(jnp.float32)
        for coef in PASS_COEFS:
            flux = weight[0] * (east(f) - f)
            for i in range(1, 4):
                flux = flux + weight[i] * (sides[i](f) - f)
            f = f + coef * flux
        f = (weight[4] * f).astype(jnp.bfloat16).astype(jnp.float32)
        turned = f.T
        for g in range(groups):
            at = pl.multiple_of(modes_rows + (t * groups + g) * own, own)
            block = turned[g * win + HALO : g * win + HALO + own, :]
            for c in range(nx // LANES):
                stack[c, pl.ds(at, own), :] = block[:, c * LANES : (c + 1) * LANES]

    for fy in range(fy_count):
        for c in range(nx // LANES):
            at = fy * nx + c * LANES
            rows_ref[:, at : at + LANES] = stack[c, pl.ds(fy, total_rows, stride=fy_count), :].astype(jnp.bfloat16)
    gram_ref[...] = jnp.zeros_like(gram_ref)
    gram_ref[:, 0:total_rows] = lax.dot_general(
        rows_ref[...], rows_ref[...], (((1,), (1,)), ((), ())), preferred_element_type=jnp.float32
    )


def solve_kernel(total_cells, nx, gram_ref, weights_ref, rows_ref, basis_ref, coef_ref, k_t, full, out):
    modes = weights_ref.shape[1]
    total_rows = gram_ref.shape[0]
    fy_count = rows_ref.shape[1] // nx
    eye = (
        lax.broadcasted_iota(jnp.int32, (modes, modes), 0) == lax.broadcasted_iota(jnp.int32, (modes, modes), 1)
    )
    full[...] = jnp.zeros_like(full)
    full[0:total_rows, :] = gram_ref[...]
    coefficients = full[modes:total_rows, 0:modes] * (1.0 / math.sqrt(total_cells))
    coef_ref[...] = coefficients
    k_t[...] = jnp.zeros_like(k_t)
    k_t[0:modes, 0:modes] = jnp.where(eye, weights_ref[...], 0.0)
    k_t[modes:total_rows, 0:modes] = coefficients.astype(jnp.bfloat16).astype(jnp.float32)
    k = k_t[...].T
    half = jnp.dot(full[...], k_t[...], precision=HIGH, preferred_element_type=jnp.float32)
    gram = jnp.dot(k, half, precision=HIGH, preferred_element_type=jnp.float32)[0:modes, 0:modes] * (1.0 / total_cells)

    a = jnp.concatenate([gram, jnp.where(eye, 1.0, 0.0)], axis=1)
    done = []
    for j in range(modes):
        top = j % 8
        row = a[top : top + 1, :]
        factor = a[:, j : j + 1] * (1.0 / row[:, j : j + 1])
        below = lax.broadcasted_iota(jnp.int32, (a.shape[0], 1), 0) > top
        a = a - jnp.where(below, factor, 0.0) * row
        if top == 7:
            done.append(a[0:8, :])
            a = a[8:, :]
    a = jnp.concatenate(done, axis=0)
    diagonal = jnp.sum(jnp.where(eye, a[:, 0:modes], 0.0), axis=1, keepdims=True)
    inverse = a[:, modes : 2 * modes] * (1.0 / jnp.sqrt(diagonal))
    mix = jnp.dot(inverse, k[0:modes, :], precision=HIGH, preferred_element_type=jnp.float32)[:, 0:total_rows]
    high = mix.astype(jnp.bfloat16)
    low = (mix - high.astype(jnp.float32)).astype(jnp.bfloat16)
    for fy in range(fy_count):
        block = rows_ref[:, fy * nx : (fy + 1) * nx]
        solved = jnp.dot(high, block, preferred_element_type=jnp.float32) + jnp.dot(
            low, block, preferred_element_type=jnp.float32
        )
        for c in range(nx // LANES):
            out[c, pl.ds(fy, modes, stride=fy_count), :] = solved[:, c * LANES : (c + 1) * LANES]
    for c in range(nx // LANES):
        basis_ref[:, c * LANES : (c + 1) * LANES] = out[c].astype(jnp.bfloat16)


def params(limit, collective_id=None):
    if collective_id is None:
        return pltpu.CompilerParams(vmem_limit_bytes=limit)
    return pltpu.CompilerParams(vmem_limit_bytes=limit, collective_id=collective_id, has_side_effects=True)


def local(n, snapshots, basis, mode_weights, land_mask, scale_index, scale_values):
    snaps, fields, cols, ny = snapshots.shape
    modes, _, own, nx = basis.shape
    win = own + 2 * HALO
    groups = LANES // win
    tiles = snaps * fields // groups
    fy_count = fields * own
    total_rows = modes + snaps
    total_cells = float(fields * nx * ny)
    limit = 48 * 1024 * 1024

    mask = jnp.broadcast_to(land_mask.astype(jnp.bfloat16)[None], (groups, cols, ny))
    pieces = jnp.concatenate([snapshots.reshape(tiles * groups, cols, ny), mask], axis=0)
    pieces = pieces.reshape(tiles + 1, groups, cols, ny)
    y = lax.broadcasted_iota(jnp.int32, (ny, n * LANES), 0)
    column = lax.broadcasted_iota(jnp.int32, (ny, n * LANES), 1)
    target, lane = column // LANES, column % LANES
    choices = []
    for g in range(groups):
        here = (lane >= g * win) & (lane < (g + 1) * win)
        choices.append((here & (y == target * own - HALO + lane - g * win)).astype(jnp.bfloat16))
    send = lax.dot_general(
        jnp.swapaxes(pieces, 1, 2).reshape((tiles + 1) * cols, groups * ny),
        jnp.concatenate(choices, axis=0),
        (((1,), (0,)), ((), ())),
        preferred_element_type=jnp.float32,
    ).astype(jnp.bfloat16).reshape(tiles + 1, cols, n * LANES)

    sems = [pltpu.SemaphoreType.DMA((n,)), pltpu.SemaphoreType.DMA((n,))]
    recv = pl.pallas_call(
        functools.partial(spread_kernel, n, cols),
        out_shape=jax.ShapeDtypeStruct((tiles + 1, nx, LANES), jnp.bfloat16),
        in_specs=[VMEM],
        out_specs=VMEM,
        scratch_shapes=[pltpu.VMEM((tiles + 1, nx, LANES), jnp.bfloat16)] + sems,
        compiler_params=params(limit, 0),
        name="spread",
    )(send)
    rows, part = pl.pallas_call(
        functools.partial(filter_kernel, win, groups),
        out_shape=(
            jax.ShapeDtypeStruct((total_rows, fy_count * nx), jnp.bfloat16),
            jax.ShapeDtypeStruct((total_rows, LANES), jnp.float32),
        ),
        in_specs=[VMEM] * 4,
        out_specs=(VMEM, VMEM),
        scratch_shapes=[
            pltpu.VMEM((nx // LANES, total_rows * fy_count, LANES), jnp.float32),
            pltpu.VMEM((5, nx, LANES), jnp.float32),
        ],
        compiler_params=params(limit),
        name="filter",
    )(recv, basis.reshape(modes * fy_count, nx), scale_index.reshape(1, ny), scale_values.reshape(1, -1))
    total = pl.pallas_call(
        functools.partial(sum_kernel, n),
        out_shape=jax.ShapeDtypeStruct((total_rows, LANES), jnp.float32),
        in_specs=[VMEM],
        out_specs=VMEM,
        scratch_shapes=[pltpu.VMEM((n, total_rows, LANES), jnp.float32)] + sems,
        compiler_params=params(limit, 1),
        name="total",
    )(part)
    new_basis, coefficients = pl.pallas_call(
        functools.partial(solve_kernel, total_cells, nx),
        out_shape=(
            jax.ShapeDtypeStruct((modes * fy_count, nx), jnp.bfloat16),
            jax.ShapeDtypeStruct((snaps, modes), jnp.float32),
        ),
        in_specs=[VMEM] * 3,
        out_specs=(VMEM, VMEM),
        scratch_shapes=[
            pltpu.VMEM((LANES, LANES), jnp.float32),
            pltpu.VMEM((LANES, LANES), jnp.float32),
            pltpu.VMEM((nx // LANES, modes * fy_count, LANES), jnp.float32),
        ],
        compiler_params=params(limit),
        name="solve",
    )(total, mode_weights.reshape(1, modes), rows)
    return new_basis.reshape(basis.shape), coefficients


def solution(mesh):
    placed = (
        P("group", None, "space", None),
        P("group", None, "space", None),
        P("group"),
        P("space", None),
        P(),
        P(),
    )
    return jax.shard_map(
        functools.partial(local, mesh.shape["space"]),
        mesh=mesh,
        in_specs=placed,
        out_specs=(P("group", None, "space", None), P("group", None)),
        check_vma=False,
    )
```

```python
import functools
import math

import jax
import jax.numpy as jnp
from jax import lax
from jax.experimental import pallas as pl
from jax.experimental.pallas import tpu as pltpu
from jax.sharding import PartitionSpec as P

PASS_COEFS = (1.0, 0.95, 0.85, 0.7, 0.5, 0.3)
HALO = len(PASS_COEFS)
LANES = 128
HIGH = lax.Precision.HIGHEST
MESH = pl.DeviceIdType.MESH
VMEM = pl.BlockSpec(memory_space=pltpu.VMEM)


def peer(step, n):
    return lax.rem(lax.axis_index("space") + step, n)


def greet(n):
    group = lax.axis_index("group")
    barrier = pltpu.get_barrier_semaphore()

    def signal(step, carry):
        pl.semaphore_signal(barrier, inc=1, device_id=(group, peer(step, n)), device_id_type=MESH)
        return carry

    lax.fori_loop(1, n, signal, 0)
    pl.semaphore_wait(barrier, n - 1)


def exchange(n, make_copy):
    def start(step, carry):
        make_copy(peer(step, n), lax.axis_index("space")).start()
        return carry

    def wait_recv(step, carry):
        source = peer(n - step, n)
        make_copy(source, source).wait_recv()
        return carry

    def wait_send(step, carry):
        make_copy(peer(step, n), lax.axis_index("space")).wait_send()
        return carry

    lax.fori_loop(1, n, start, 0)
    return lambda: lax.fori_loop(1, n, wait_recv, 0), lambda: lax.fori_loop(1, n, wait_send, 0)


def spread_kernel(n, cols, send_ref, recv_ref, land, send_sem, recv_sem):
    me = lax.axis_index("space")
    group = lax.axis_index("group")
    greet(n)

    def make_copy(dst, slot):
        return pltpu.make_async_remote_copy(
            src_ref=send_ref.at[:, :, pl.ds(pl.multiple_of(dst * LANES, LANES), LANES)],
            dst_ref=land.at[:, pl.ds(pl.multiple_of(slot * cols, cols), cols), :],
            send_sem=send_sem.at[dst],
            recv_sem=recv_sem.at[slot],
            device_id=(group, dst),
            device_id_type=MESH,
        )

    arrived, sent = exchange(n, make_copy)
    land[:, pl.ds(pl.multiple_of(me * cols, cols), cols), :] = send_ref[
        :, :, pl.ds(pl.multiple_of(me * LANES, LANES), LANES)
    ]
    arrived()
    recv_ref[...] = land[...]
    sent()


def sum_kernel(n, part_ref, total_ref, land, gather, send_part, recv_part, send_sum, recv_sum):
    me = lax.axis_index("space")
    group = lax.axis_index("group")
    bands = part_ref.shape[0] // 8
    mine = lax.div(me * bands + n - 1, n)

    def owner(band):
        return lax.div(band * n, bands)

    def band_rows(band):
        return pl.ds(pl.multiple_of(band * 8, 8), 8)

    def part_copy(band, slot):
        return pltpu.make_async_remote_copy(
            src_ref=part_ref.at[band_rows(band)],
            dst_ref=land.at[slot],
            send_sem=send_part.at[band],
            recv_sem=recv_part.at[slot],
            device_id=(group, owner(band)),
            device_id_type=MESH,
        )

    def sum_copy(band, dst):
        return pltpu.make_async_remote_copy(
            src_ref=gather.at[band_rows(band)],
            dst_ref=gather.at[band_rows(band)],
            send_sem=send_sum.at[dst],
            recv_sem=recv_sum.at[band],
            device_id=(group, dst),
            device_id_type=MESH,
        )

    def others(act):
        def body(band, carry):
            @pl.when(owner(band) != me)
            def _():
                act(band)

            return carry

        lax.fori_loop(0, bands, body, 0)

    def peers(act):
        def body(step, carry):
            act(peer(step, n))
            return carry

        lax.fori_loop(1, n, body, 0)

    greet(n)
    others(lambda band: part_copy(band, me).start())
    owns = (mine < bands) & (owner(mine) == me)

    @pl.when(owns)
    def _():
        land[me] = part_ref[band_rows(mine)]
        peers(lambda source: part_copy(mine, source).wait_recv())
        total = land[0]
        for slot in range(1, n):
            total = total + land[slot]
        gather[band_rows(mine), :] = total
        peers(lambda dst: sum_copy(mine, dst).start())

    others(lambda band: sum_copy(band, me).wait_recv())
    total_ref[...] = gather[...]
    others(lambda band: part_copy(band, me).wait_send())

    @pl.when(owns)
    def _():
        peers(lambda dst: sum_copy(mine, dst).wait_send())


def filter_kernel(win, groups, recv_ref, basis_ref, index_ref, values_ref, rows_ref, gram_ref, stack, weight):
    tiles = recv_ref.shape[0] - 1
    nx = recv_ref.shape[1]
    own = win - 2 * HALO
    ny = index_ref.shape[1]
    modes_rows = basis_ref.shape[0]
    total_rows, fy_count = rows_ref.shape[0], rows_ref.shape[1] // nx
    me = lax.axis_index("space")

    for c in range(nx // LANES):
        stack[c, 0:modes_rows, :] = basis_ref[:, c * LANES : (c + 1) * LANES].astype(jnp.float32)

    lat = jnp.zeros((1, ny), jnp.float32)
    for level in range(values_ref.shape[1]):
        lat = lat + jnp.where(index_ref[...] == level, values_ref[0:1, level : level + 1], 0.0)
    lane = lax.broadcasted_iota(jnp.int32, (ny, LANES), 1)
    row = lax.broadcasted_iota(jnp.int32, (ny, LANES), 0)
    pick = jnp.zeros((ny, LANES), jnp.float32)
    for g in range(groups):
        here = (lane >= g * win) & (lane < (g + 1) * win)
        pick = jnp.where(here & (row == me * own - HALO + lane - g * win), 1.0, pick)
    lat_lane = jnp.dot(jnp.broadcast_to(lat, (8, ny)), pick, precision=HIGH, preferred_element_type=jnp.float32)[0:1]

    def east(a):
        return pltpu.roll(a, nx - 1, 0)

    def west(a):
        return pltpu.roll(a, 1, 0)

    def north(a):
        return pltpu.roll(a, LANES - 1, 1)

    def south(a):
        return pltpu.roll(a, 1, 1)

    ocean = recv_ref[tiles].astype(jnp.float32)
    base = ocean * lat_lane
    sides = (east, west, north, south)
    for i, side in enumerate(sides):
        weight[i] = base * side(ocean)
    weight[4] = ocean

    @pl.loop(0, tiles)
    def _(t):
        f = recv_ref[t].astype(jnp.float32)
        for coef in PASS_COEFS:
            flux = weight[0] * (east(f) - f)
            for i in range(1, 4):
                flux = flux + weight[i] * (sides[i](f) - f)
            f = f + coef * flux
        f = (weight[4] * f).astype(jnp.bfloat16).astype(jnp.float32)
        turned = f.T
        for g in range(groups):
            at = pl.multiple_of(modes_rows + (t * groups + g) * own, own)
            block = turned[g * win + HALO : g * win + HALO + own, :]
            for c in range(nx // LANES):
                stack[c, pl.ds(at, own), :] = block[:, c * LANES : (c + 1) * LANES]

    for fy in range(fy_count):
        for c in range(nx // LANES):
            at = fy * nx + c * LANES
            rows_ref[:, at : at + LANES] = stack[c, pl.ds(fy, total_rows, stride=fy_count), :].astype(jnp.bfloat16)
    gram_ref[...] = jnp.zeros_like(gram_ref)
    gram_ref[:, 0:total_rows] = lax.dot_general(
        rows_ref[...], rows_ref[...], (((1,), (1,)), ((), ())), preferred_element_type=jnp.float32
    )


def solve_kernel(total_cells, nx, gram_ref, weights_ref, rows_ref, basis_ref, coef_ref, k_t, full, out):
    modes = weights_ref.shape[1]
    total_rows = gram_ref.shape[0]
    fy_count = rows_ref.shape[1] // nx
    eye = (
        lax.broadcasted_iota(jnp.int32, (modes, modes), 0) == lax.broadcasted_iota(jnp.int32, (modes, modes), 1)
    )
    full[...] = jnp.zeros_like(full)
    full[0:total_rows, :] = gram_ref[...]
    coefficients = full[modes:total_rows, 0:modes] * (1.0 / math.sqrt(total_cells))
    coef_ref[...] = coefficients
    k_t[...] = jnp.zeros_like(k_t)
    k_t[0:modes, 0:modes] = jnp.where(eye, weights_ref[...], 0.0)
    k_t[modes:total_rows, 0:modes] = coefficients.astype(jnp.bfloat16).astype(jnp.float32)
    k = k_t[...].T
    half = jnp.dot(full[...], k_t[...], precision=HIGH, preferred_element_type=jnp.float32)
    gram = jnp.dot(k, half, precision=HIGH, preferred_element_type=jnp.float32)[0:modes, 0:modes] * (1.0 / total_cells)

    a = jnp.concatenate([gram, jnp.where(eye, 1.0, 0.0)], axis=1)
    done = []
    for j in range(modes):
        top = j % 8
        row = a[top : top + 1, :]
        factor = a[:, j : j + 1] * (1.0 / row[:, j : j + 1])
        below = lax.broadcasted_iota(jnp.int32, (a.shape[0], 1), 0) > top
        a = a - jnp.where(below, factor, 0.0) * row
        if top == 7:
            done.append(a[0:8, :])
            a = a[8:, :]
    a = jnp.concatenate(done, axis=0)
    diagonal = jnp.sum(jnp.where(eye, a[:, 0:modes], 0.0), axis=1, keepdims=True)
    inverse = a[:, modes : 2 * modes] * (1.0 / jnp.sqrt(diagonal))
    mix = jnp.dot(inverse, k[0:modes, :], precision=HIGH, preferred_element_type=jnp.float32)[:, 0:total_rows]
    high = mix.astype(jnp.bfloat16)
    low = (mix - high.astype(jnp.float32)).astype(jnp.bfloat16)
    for fy in range(fy_count):
        block = rows_ref[:, fy * nx : (fy + 1) * nx]
        solved = jnp.dot(high, block, preferred_element_type=jnp.float32) + jnp.dot(
            low, block, preferred_element_type=jnp.float32
        )
        for c in range(nx // LANES):
            out[c, pl.ds(fy, modes, stride=fy_count), :] = solved[:, c * LANES : (c + 1) * LANES]
    for c in range(nx // LANES):
        basis_ref[:, c * LANES : (c + 1) * LANES] = out[c].astype(jnp.bfloat16)


def params(limit, collective_id=None):
    if collective_id is None:
        return pltpu.CompilerParams(vmem_limit_bytes=limit)
    return pltpu.CompilerParams(vmem_limit_bytes=limit, collective_id=collective_id, has_side_effects=True)


def local(n, snapshots, basis, mode_weights, land_mask, scale_index, scale_values):
    snaps, fields, cols, ny = snapshots.shape
    modes, _, own, nx = basis.shape
    win = own + 2 * HALO
    groups = LANES // win
    tiles = snaps * fields // groups
    fy_count = fields * own
    total_rows = modes + snaps
    total_cells = float(fields * nx * ny)
    limit = 48 * 1024 * 1024

    mask = jnp.broadcast_to(land_mask.astype(jnp.bfloat16)[None], (groups, cols, ny))
    pieces = jnp.concatenate([snapshots.reshape(tiles * groups, cols, ny), mask], axis=0)
    pieces = pieces.reshape(tiles + 1, groups, cols, ny)
    y = lax.broadcasted_iota(jnp.int32, (ny, n * LANES), 0)
    column = lax.broadcasted_iota(jnp.int32, (ny, n * LANES), 1)
    target, lane = column // LANES, column % LANES
    choices = []
    for g in range(groups):
        here = (lane >= g * win) & (lane < (g + 1) * win)
        choices.append((here & (y == target * own - HALO + lane - g * win)).astype(jnp.bfloat16))
    send = lax.dot_general(
        jnp.swapaxes(pieces, 1, 2).reshape((tiles + 1) * cols, groups * ny),
        jnp.concatenate(choices, axis=0),
        (((1,), (0,)), ((), ())),
        preferred_element_type=jnp.float32,
    ).astype(jnp.bfloat16).reshape(tiles + 1, cols, n * LANES)

    sems = [pltpu.SemaphoreType.DMA((n,)), pltpu.SemaphoreType.DMA((n,))]
    recv = pl.pallas_call(
        functools.partial(spread_kernel, n, cols),
        out_shape=jax.ShapeDtypeStruct((tiles + 1, nx, LANES), jnp.bfloat16),
        in_specs=[VMEM],
        out_specs=VMEM,
        scratch_shapes=[pltpu.VMEM((tiles + 1, nx, LANES), jnp.bfloat16)] + sems,
        compiler_params=params(limit, 0),
        name="spread",
    )(send)
    rows, part = pl.pallas_call(
        functools.partial(filter_kernel, win, groups),
        out_shape=(
            jax.ShapeDtypeStruct((total_rows, fy_count * nx), jnp.bfloat16),
            jax.ShapeDtypeStruct((total_rows, LANES), jnp.float32),
        ),
        in_specs=[VMEM] * 4,
        out_specs=(VMEM, VMEM),
        scratch_shapes=[
            pltpu.VMEM((nx // LANES, total_rows * fy_count, LANES), jnp.float32),
            pltpu.VMEM((5, nx, LANES), jnp.float32),
        ],
        compiler_params=params(limit),
        name="filter",
    )(recv, basis.reshape(modes * fy_count, nx), scale_index.reshape(1, ny), scale_values.reshape(1, -1))
    total = pl.pallas_call(
        functools.partial(sum_kernel, n),
        out_shape=jax.ShapeDtypeStruct((total_rows, LANES), jnp.float32),
        in_specs=[VMEM],
        out_specs=VMEM,
        scratch_shapes=[
            pltpu.VMEM((n, 8, LANES), jnp.float32),
            pltpu.VMEM((total_rows, LANES), jnp.float32),
            pltpu.SemaphoreType.DMA((total_rows // 8,)),
            pltpu.SemaphoreType.DMA((n,)),
            pltpu.SemaphoreType.DMA((n,)),
            pltpu.SemaphoreType.DMA((total_rows // 8,)),
        ],
        compiler_params=params(limit, 1),
        name="total",
    )(part)
    new_basis, coefficients = pl.pallas_call(
        functools.partial(solve_kernel, total_cells, nx),
        out_shape=(
            jax.ShapeDtypeStruct((modes * fy_count, nx), jnp.bfloat16),
            jax.ShapeDtypeStruct((snaps, modes), jnp.float32),
        ),
        in_specs=[VMEM] * 3,
        out_specs=(VMEM, VMEM),
        scratch_shapes=[
            pltpu.VMEM((LANES, LANES), jnp.float32),
            pltpu.VMEM((LANES, LANES), jnp.float32),
            pltpu.VMEM((nx // LANES, modes * fy_count, LANES), jnp.float32),
        ],
        compiler_params=params(limit),
        name="solve",
    )(total, mode_weights.reshape(1, modes), rows)
    return new_basis.reshape(basis.shape), coefficients


def solution(mesh):
    placed = (
        P("group", None, "space", None),
        P("group", None, "space", None),
        P("group"),
        P("space", None),
        P(),
        P(),
    )
    return jax.shard_map(
        functools.partial(local, mesh.shape["space"]),
        mesh=mesh,
        in_specs=placed,
        out_specs=(P("group", None, "space", None), P("group", None)),
        check_vma=False,
    )
```

```python
import functools
import math

import jax
import jax.numpy as jnp
from jax import lax
from jax.experimental import pallas as pl
from jax.experimental.pallas import tpu as pltpu
from jax.sharding import PartitionSpec as P

PASS_COEFS = (1.0, 0.95, 0.85, 0.7, 0.5, 0.3)
HALO = len(PASS_COEFS)
LANES = 128
HIGH = lax.Precision.HIGHEST
MESH = pl.DeviceIdType.MESH
VMEM = pl.BlockSpec(memory_space=pltpu.VMEM)


def peer(step, n):
    return lax.rem(lax.axis_index("space") + step, n)


def greet(n):
    group = lax.axis_index("group")
    barrier = pltpu.get_barrier_semaphore()

    def signal(step, carry):
        pl.semaphore_signal(barrier, inc=1, device_id=(group, peer(step, n)), device_id_type=MESH)
        return carry

    lax.fori_loop(1, n, signal, 0)
    pl.semaphore_wait(barrier, n - 1)


def band_sum(n, part_ref, total_ref, land, gather, send_part, recv_part, send_sum, recv_sum):
    me = lax.axis_index("space")
    group = lax.axis_index("group")
    bands = part_ref.shape[0] // 8
    mine = lax.div(me * bands + n - 1, n)

    def owner(band):
        return lax.div(band * n, bands)

    def band_rows(band):
        return pl.ds(pl.multiple_of(band * 8, 8), 8)

    def part_copy(band, slot):
        return pltpu.make_async_remote_copy(
            src_ref=part_ref.at[band_rows(band)],
            dst_ref=land.at[slot],
            send_sem=send_part.at[band],
            recv_sem=recv_part.at[slot],
            device_id=(group, owner(band)),
            device_id_type=MESH,
        )

    def sum_copy(band, dst):
        return pltpu.make_async_remote_copy(
            src_ref=gather.at[band_rows(band)],
            dst_ref=gather.at[band_rows(band)],
            send_sem=send_sum.at[dst],
            recv_sem=recv_sum.at[band],
            device_id=(group, dst),
            device_id_type=MESH,
        )

    def others(act):
        def body(band, carry):
            @pl.when(owner(band) != me)
            def _():
                act(band)

            return carry

        lax.fori_loop(0, bands, body, 0)

    def peers(act):
        def body(step, carry):
            act(peer(step, n))
            return carry

        lax.fori_loop(1, n, body, 0)

    others(lambda band: part_copy(band, me).start())
    owns = (mine < bands) & (owner(mine) == me)

    @pl.when(owns)
    def _():
        land[me] = part_ref[band_rows(mine)]
        peers(lambda source: part_copy(mine, source).wait_recv())
        total = land[0]
        for slot in range(1, n):
            total = total + land[slot]
        gather[band_rows(mine), :] = total
        peers(lambda dst: sum_copy(mine, dst).start())

    others(lambda band: sum_copy(band, me).wait_recv())
    total_ref[...] = gather[...]
    others(lambda band: part_copy(band, me).wait_send())

    @pl.when(owns)
    def _():
        peers(lambda dst: sum_copy(mine, dst).wait_send())


def swap_groups(parts, width):
    parts = list(parts)
    size = parts[0].shape[1]
    lane = lax.broadcasted_iota(jnp.int32, parts[0].shape, 1)
    bit = 1
    while bit < len(parts):
        shift = bit * width
        upper = lax.rem(lax.div(lane, shift), 2) == 1
        for s in range(len(parts)):
            if not s & bit:
                a, b = parts[s], parts[s | bit]
                parts[s] = jnp.where(upper, pltpu.roll(b, shift, 1), a)
                parts[s | bit] = jnp.where(upper, b, pltpu.roll(a, size - shift, 1))
        bit *= 2
    return parts


def project_kernel(
    n,
    cols,
    snaps_ref,
    mask_ref,
    basis_ref,
    index_ref,
    values_ref,
    rows_ref,
    total_ref,
    wide,
    spread,
    weight,
    packed,
    land,
    stack,
    part,
    band_land,
    gather,
    edge_send,
    edge_recv,
    data_send,
    data_recv,
    send_part,
    recv_part,
    send_sum,
    recv_sum,
):
    me = lax.axis_index("space")
    group = lax.axis_index("group")
    count = snaps_ref.shape[0] // cols
    ny, nx = snaps_ref.shape[1], basis_ref.shape[1]
    own = ny // n
    groups = LANES // own
    modes_rows = basis_ref.shape[0]
    total_rows, fy_count = rows_ref.shape[0], rows_ref.shape[1] // nx
    modes = modes_rows // fy_count
    y_tiles, x_tiles = ny // LANES, nx // LANES

    for c in range(y_tiles):
        spread[c] = snaps_ref[:, c * LANES : (c + 1) * LANES].astype(jnp.float32)
    for x in range(cols):
        for c in range(y_tiles):
            wide[HALO + x, 0:count, c * LANES : (c + 1) * LANES] = spread[
                c, pl.ds(x, count, stride=cols), :
            ].astype(jnp.bfloat16)
        line = mask_ref[x : x + 1, :].astype(jnp.float32)
        wide[HALO + x, count : count + 16, :] = jnp.broadcast_to(line, (16, ny)).astype(jnp.bfloat16)

    greet(n)

    def edge_copy(first, to, where, who):
        return pltpu.make_async_remote_copy(
            src_ref=wide.at[pl.ds(first, HALO)],
            dst_ref=wide.at[pl.ds(to, HALO)],
            send_sem=edge_send.at[where],
            recv_sem=edge_recv.at[where],
            device_id=(group, who),
            device_id_type=MESH,
        )

    to_left = edge_copy(HALO, HALO + cols, 0, peer(n - 1, n))
    to_right = edge_copy(cols, 0, 1, peer(1, n))
    to_left.start()
    to_right.start()

    for c in range(x_tiles):
        stack[c, 0:modes_rows, :] = basis_ref[:, c * LANES : (c + 1) * LANES].astype(jnp.float32)
    for fy in range(fy_count):
        for c in range(x_tiles):
            at = fy * nx + c * LANES
            rows_ref[0:modes, at : at + LANES] = stack[c, pl.ds(fy, modes, stride=fy_count), :].astype(jnp.bfloat16)
    part[...] = jnp.zeros_like(part)
    part[0:modes, 0:modes] = lax.dot_general(
        rows_ref[0:modes, :], rows_ref[0:modes, :], (((1,), (1,)), ((), ())), preferred_element_type=jnp.float32
    )
    lat = jnp.zeros((1, ny), jnp.float32)
    for level in range(values_ref.shape[1]):
        lat = lat + jnp.where(index_ref[...] == level, values_ref[0:1, level : level + 1], 0.0)
    lane = lax.broadcasted_iota(jnp.int32, (8, ny), 1)

    to_left.wait()
    to_right.wait()

    def north(a):
        return pltpu.roll(a, ny - 1, 1)

    def south(a):
        return pltpu.roll(a, 1, 1)

    last = cols + 2 * HALO
    ocean = [wide[x, count : count + 16, :].astype(jnp.float32)[0:8] for x in range(last)]
    for x in range(1, last - 1):
        base = ocean[x] * lat
        weight[0, x] = base * ocean[x + 1]
        weight[1, x] = base * ocean[x - 1]
        weight[2, x] = jnp.where(lane == ny - 1, 0.0, base * north(ocean[x]))
        weight[3, x] = jnp.where(lane == 0, 0.0, base * south(ocean[x]))
        weight[4, x] = ocean[x]

    @pl.loop(0, count // 16)
    def _(block):
        start = pl.multiple_of(block * 16, 16)
        both = [wide[x, pl.ds(start, 16), :].astype(jnp.float32) for x in range(last)]
        for side in range(2):
            f = [b[side * 8 : side * 8 + 8] for b in both]
            for i, coef in enumerate(PASS_COEFS):
                new = list(f)
                for x in range(i + 1, last - i - 1):
                    centre = f[x]
                    flux = weight[0, x] * (f[x + 1] - centre) + weight[1, x] * (f[x - 1] - centre)
                    flux = flux + weight[2, x] * (north(centre) - centre) + weight[3, x] * (south(centre) - centre)
                    new[x] = centre + coef * flux
                f = new
            for x in range(cols):
                done = weight[4, HALO + x] * f[HALO + x]
                at = pl.multiple_of(x * count + start + side * 8, 8)
                for c in range(y_tiles):
                    spread[c, pl.ds(at, 8), :] = done[:, c * LANES : (c + 1) * LANES]

    for t in range(count // groups):
        for c in range(y_tiles):
            parts = [spread[c, pl.ds(t * groups + g, cols, stride=count), :] for g in range(groups)]
            for g, piece in enumerate(swap_groups(parts, own)):
                packed[c * groups + g, t] = piece.astype(jnp.bfloat16)

    def data_copy(dst, slot):
        return pltpu.make_async_remote_copy(
            src_ref=packed.at[dst],
            dst_ref=land.at[:, pl.ds(pl.multiple_of(slot * cols, cols), cols), :],
            send_sem=data_send.at[dst],
            recv_sem=data_recv.at[slot],
            device_id=(group, dst),
            device_id_type=MESH,
        )

    def each_peer(act):
        def body(step, carry):
            act(peer(step, n))
            return carry

        lax.fori_loop(1, n, body, 0)

    each_peer(lambda dst: data_copy(dst, me).start())
    land[:, pl.ds(pl.multiple_of(me * cols, cols), cols), :] = packed[me]
    each_peer(lambda source: data_copy(source, source).wait_recv())

    for t in range(count // groups):
        turned = land[t].astype(jnp.float32).T
        for c in range(x_tiles):
            stack[c, modes_rows + t * LANES : modes_rows + (t + 1) * LANES, :] = turned[:, c * LANES : (c + 1) * LANES]
    for fy in range(fy_count):
        for c in range(x_tiles):
            at = fy * nx + c * LANES
            rows_ref[modes:total_rows, at : at + LANES] = stack[
                c, pl.ds(modes_rows + fy, total_rows - modes, stride=fy_count), :
            ].astype(jnp.bfloat16)
    part[modes:total_rows, 0:total_rows] = lax.dot_general(
        rows_ref[modes:total_rows, :], rows_ref[...], (((1,), (1,)), ((), ())), preferred_element_type=jnp.float32
    )
    band_sum(n, part, total_ref, band_land, gather, send_part, recv_part, send_sum, recv_sum)
    each_peer(lambda dst: data_copy(dst, me).wait_send())


def solve_kernel(total_cells, nx, gram_ref, weights_ref, rows_ref, basis_ref, coef_ref, k_t, full, out):
    modes = weights_ref.shape[1]
    total_rows = gram_ref.shape[0]
    fy_count = rows_ref.shape[1] // nx
    eye = (
        lax.broadcasted_iota(jnp.int32, (modes, modes), 0) == lax.broadcasted_iota(jnp.int32, (modes, modes), 1)
    )
    full[...] = jnp.zeros_like(full)
    full[0:total_rows, :] = gram_ref[...]
    row = lax.broadcasted_iota(jnp.int32, full.shape, 0)
    column = lax.broadcasted_iota(jnp.int32, full.shape, 1)
    full[...] = jnp.where((row < modes) & (column >= modes), full[...].T, full[...])
    coefficients = full[modes:total_rows, 0:modes] * (1.0 / math.sqrt(total_cells))
    coef_ref[...] = coefficients
    k_t[...] = jnp.zeros_like(k_t)
    k_t[0:modes, 0:modes] = jnp.where(eye, weights_ref[...], 0.0)
    k_t[modes:total_rows, 0:modes] = coefficients.astype(jnp.bfloat16).astype(jnp.float32)
    k = k_t[...].T
    half = jnp.dot(full[...], k_t[...], precision=HIGH, preferred_element_type=jnp.float32)
    gram = jnp.dot(k, half, precision=HIGH, preferred_element_type=jnp.float32)[0:modes, 0:modes] * (1.0 / total_cells)

    a = jnp.concatenate([gram, jnp.where(eye, 1.0, 0.0)], axis=1)
    done = []
    for j in range(modes):
        top = j % 8
        row = a[top : top + 1, :]
        factor = a[:, j : j + 1] * (1.0 / row[:, j : j + 1])
        below = lax.broadcasted_iota(jnp.int32, (a.shape[0], 1), 0) > top
        a = a - jnp.where(below, factor, 0.0) * row
        if top == 7:
            done.append(a[0:8, :])
            a = a[8:, :]
    a = jnp.concatenate(done, axis=0)
    diagonal = jnp.sum(jnp.where(eye, a[:, 0:modes], 0.0), axis=1, keepdims=True)
    inverse = a[:, modes : 2 * modes] * (1.0 / jnp.sqrt(diagonal))
    mix = jnp.dot(inverse, k[0:modes, :], precision=HIGH, preferred_element_type=jnp.float32)[:, 0:total_rows]
    high = mix.astype(jnp.bfloat16)
    low = (mix - high.astype(jnp.float32)).astype(jnp.bfloat16)
    for fy in range(fy_count):
        block = rows_ref[:, fy * nx : (fy + 1) * nx]
        solved = jnp.dot(high, block, preferred_element_type=jnp.float32) + jnp.dot(
            low, block, preferred_element_type=jnp.float32
        )
        for c in range(nx // LANES):
            out[c, pl.ds(fy, modes, stride=fy_count), :] = solved[:, c * LANES : (c + 1) * LANES]
    for c in range(nx // LANES):
        basis_ref[:, c * LANES : (c + 1) * LANES] = out[c].astype(jnp.bfloat16)


def params(limit, collective_id=None):
    if collective_id is None:
        return pltpu.CompilerParams(vmem_limit_bytes=limit)
    return pltpu.CompilerParams(vmem_limit_bytes=limit, collective_id=collective_id, has_side_effects=True)


def local(n, snapshots, basis, mode_weights, land_mask, scale_index, scale_values):
    snaps, fields, cols, ny = snapshots.shape
    modes, _, own, nx = basis.shape
    count = snaps * fields
    fy_count = fields * own
    total_rows = modes + snaps
    total_cells = float(fields * nx * ny)
    limit = 48 * 1024 * 1024
    groups = LANES // own
    bands = total_rows // 8

    rows, total = pl.pallas_call(
        functools.partial(project_kernel, n, cols),
        out_shape=(
            jax.ShapeDtypeStruct((total_rows, fy_count * nx), jnp.bfloat16),
            jax.ShapeDtypeStruct((total_rows, LANES), jnp.float32),
        ),
        in_specs=[VMEM] * 5,
        out_specs=(VMEM, VMEM),
        scratch_shapes=[
            pltpu.VMEM((cols + 2 * HALO, count + 16, ny), jnp.bfloat16),
            pltpu.VMEM((ny // LANES, count * cols, LANES), jnp.float32),
            pltpu.VMEM((5, cols + 2 * HALO, 8, ny), jnp.float32),
            pltpu.VMEM((n, count // groups, cols, LANES), jnp.bfloat16),
            pltpu.VMEM((count // groups, nx, LANES), jnp.bfloat16),
            pltpu.VMEM((nx // LANES, total_rows * fy_count, LANES), jnp.float32),
            pltpu.VMEM((total_rows, LANES), jnp.float32),
            pltpu.VMEM((n, 8, LANES), jnp.float32),
            pltpu.VMEM((total_rows, LANES), jnp.float32),
        ]
        + [pltpu.SemaphoreType.DMA((k,)) for k in (2, 2, n, n, bands, n, n, bands)],
        compiler_params=params(limit, 0),
        name="project",
    )(
        snapshots.reshape(count * cols, ny),
        land_mask,
        basis.reshape(modes * fy_count, nx),
        scale_index.reshape(1, ny),
        scale_values.reshape(1, -1),
    )
    new_basis, coefficients = pl.pallas_call(
        functools.partial(solve_kernel, total_cells, nx),
        out_shape=(
            jax.ShapeDtypeStruct((modes * fy_count, nx), jnp.bfloat16),
            jax.ShapeDtypeStruct((snaps, modes), jnp.float32),
        ),
        in_specs=[VMEM] * 3,
        out_specs=(VMEM, VMEM),
        scratch_shapes=[
            pltpu.VMEM((LANES, LANES), jnp.float32),
            pltpu.VMEM((LANES, LANES), jnp.float32),
            pltpu.VMEM((nx // LANES, modes * fy_count, LANES), jnp.float32),
        ],
        compiler_params=params(limit),
        name="solve",
    )(total, mode_weights.reshape(1, modes), rows)
    return new_basis.reshape(basis.shape), coefficients


def solution(mesh):
    placed = (
        P("group", None, "space", None),
        P("group", None, "space", None),
        P("group"),
        P("space", None),
        P(),
        P(),
    )
    return jax.shard_map(
        functools.partial(local, mesh.shape["space"]),
        mesh=mesh,
        in_specs=placed,
        out_specs=(P("group", None, "space", None), P("group", None)),
        check_vma=False,
    )
```

```python
import functools
import math

import jax
import jax.numpy as jnp
from jax import lax
from jax.experimental import pallas as pl
from jax.experimental.pallas import tpu as pltpu
from jax.sharding import PartitionSpec as P

PASS_COEFS = (1.0, 0.95, 0.85, 0.7, 0.5, 0.3)
HALO = len(PASS_COEFS)
LANES = 128
HIGH = lax.Precision.HIGHEST
MESH = pl.DeviceIdType.MESH
VMEM = pl.BlockSpec(memory_space=pltpu.VMEM)
HBM = pl.BlockSpec(memory_space=pltpu.HBM)


def peer(step, n):
    return lax.rem(lax.axis_index("space") + step, n)


def greet(n):
    group = lax.axis_index("group")
    barrier = pltpu.get_barrier_semaphore()

    def signal(step, carry):
        pl.semaphore_signal(barrier, inc=1, device_id=(group, peer(step, n)), device_id_type=MESH)
        return carry

    lax.fori_loop(1, n, signal, 0)
    return barrier


def band_sum(n, bands, part_ref, land, gather, send_part, recv_part, send_sum, recv_sum):
    me = lax.axis_index("space")
    group = lax.axis_index("group")
    mine = lax.div(me * bands + n - 1, n)

    def owner(band):
        return lax.div(band * n, bands)

    def band_rows(band):
        return pl.ds(pl.multiple_of(band * 8, 8), 8)

    def part_copy(band, slot):
        return pltpu.make_async_remote_copy(
            src_ref=part_ref.at[band_rows(band)],
            dst_ref=land.at[slot],
            send_sem=send_part.at[band],
            recv_sem=recv_part.at[slot],
            device_id=(group, owner(band)),
            device_id_type=MESH,
        )

    def sum_copy(band, dst):
        return pltpu.make_async_remote_copy(
            src_ref=gather.at[band_rows(band)],
            dst_ref=gather.at[band_rows(band)],
            send_sem=send_sum.at[dst],
            recv_sem=recv_sum.at[band],
            device_id=(group, dst),
            device_id_type=MESH,
        )

    def others(act):
        def body(band, carry):
            @pl.when(owner(band) != me)
            def _():
                act(band)

            return carry

        lax.fori_loop(0, bands, body, 0)

    def peers(act):
        def body(step, carry):
            act(peer(step, n))
            return carry

        lax.fori_loop(1, n, body, 0)

    owns = (mine < bands) & (owner(mine) == me)

    def start():
        others(lambda band: part_copy(band, me).start())

    def reduce():
        @pl.when(owns)
        def _():
            land[me] = part_ref[band_rows(mine)]
            peers(lambda source: part_copy(mine, source).wait_recv())
            total = land[0]
            for slot in range(1, n):
                total = total + land[slot]
            gather[band_rows(mine), :] = total
            peers(lambda dst: sum_copy(mine, dst).start())

    def finish():
        others(lambda band: sum_copy(band, me).wait_recv())
        others(lambda band: part_copy(band, me).wait_send())

        @pl.when(owns)
        def _():
            peers(lambda dst: sum_copy(mine, dst).wait_send())

    return start, reduce, finish


def swap_groups(parts, width):
    parts = list(parts)
    size = parts[0].shape[1]
    lane = lax.broadcasted_iota(jnp.int32, parts[0].shape, 1)
    bit = 1
    while bit < len(parts):
        shift = bit * width
        upper = lax.rem(lax.div(lane, shift), 2) == 1
        for s in range(len(parts)):
            if not s & bit:
                a, b = parts[s], parts[s | bit]
                parts[s] = jnp.where(upper, pltpu.roll(b, shift, 1), a)
                parts[s | bit] = jnp.where(upper, b, pltpu.roll(a, size - shift, 1))
        bit *= 2
    return parts


def project_kernel(
    n,
    cols,
    snaps_hbm,
    mask_hbm,
    basis_hbm,
    index_ref,
    values_ref,
    rows_ref,
    total_ref,
    snaps_ref,
    mask_ref,
    basis_ref,
    wide,
    spread,
    weight,
    packed,
    land,
    stack,
    part,
    band_land,
    gather,
    late,
    late_land,
    loaded,
    edge_send,
    edge_recv,
    data_send,
    data_recv,
    send_part,
    recv_part,
    send_sum,
    recv_sum,
    late_send,
    late_recv,
):
    me = lax.axis_index("space")
    group = lax.axis_index("group")
    loads = [
        pltpu.make_async_copy(src, dst, loaded.at[i])
        for i, (src, dst) in enumerate(((snaps_hbm, snaps_ref), (mask_hbm, mask_ref), (basis_hbm, basis_ref)))
    ]
    for load in loads:
        load.start()
    barrier = greet(n)
    count = snaps_ref.shape[0] // cols
    ny, nx = snaps_ref.shape[1], basis_ref.shape[1]
    own = ny // n
    groups = LANES // own
    modes_rows = basis_ref.shape[0]
    total_rows, fy_count = rows_ref.shape[0], rows_ref.shape[1] // nx
    modes = modes_rows // fy_count
    y_tiles, x_tiles = ny // LANES, nx // LANES

    loads[0].wait()
    loads[1].wait()
    for c in range(y_tiles):
        spread[c] = snaps_ref[:, c * LANES : (c + 1) * LANES].astype(jnp.float32)
    for x in range(cols):
        for c in range(y_tiles):
            wide[HALO + x, 0:count, c * LANES : (c + 1) * LANES] = spread[
                c, pl.ds(x, count, stride=cols), :
            ].astype(jnp.bfloat16)
        line = mask_ref[x : x + 1, :].astype(jnp.float32)
        wide[HALO + x, count : count + 16, :] = jnp.broadcast_to(line, (16, ny)).astype(jnp.bfloat16)

    pl.semaphore_wait(barrier, n - 1)

    def edge_copy(first, to, where, who):
        return pltpu.make_async_remote_copy(
            src_ref=wide.at[pl.ds(first, HALO)],
            dst_ref=wide.at[pl.ds(to, HALO)],
            send_sem=edge_send.at[where],
            recv_sem=edge_recv.at[where],
            device_id=(group, who),
            device_id_type=MESH,
        )

    to_left = edge_copy(HALO, HALO + cols, 0, peer(n - 1, n))
    to_right = edge_copy(cols, 0, 1, peer(1, n))
    to_left.start()
    to_right.start()

    loads[2].wait()
    for c in range(x_tiles):
        stack[c, 0:modes_rows, :] = basis_ref[:, c * LANES : (c + 1) * LANES].astype(jnp.float32)
    for fy in range(fy_count):
        for c in range(x_tiles):
            at = fy * nx + c * LANES
            rows_ref[0:modes, at : at + LANES] = stack[c, pl.ds(fy, modes, stride=fy_count), :].astype(jnp.bfloat16)
    part[...] = jnp.zeros_like(part)
    part[0:modes, 0:modes] = lax.dot_general(
        rows_ref[0:modes, :], rows_ref[0:modes, :], (((1,), (1,)), ((), ())), preferred_element_type=jnp.float32
    )
    start_bands, reduce_bands, finish_bands = band_sum(
        n, modes // 8, part, band_land, gather, send_part, recv_part, send_sum, recv_sum
    )
    start_bands()
    lat = jnp.zeros((1, ny), jnp.float32)
    for level in range(values_ref.shape[1]):
        lat = lat + jnp.where(index_ref[...] == level, values_ref[0:1, level : level + 1], 0.0)
    lane = lax.broadcasted_iota(jnp.int32, (8, ny), 1)

    to_left.wait()
    to_right.wait()

    def north(a):
        return pltpu.roll(a, ny - 1, 1)

    def south(a):
        return pltpu.roll(a, 1, 1)

    last = cols + 2 * HALO
    ocean = [wide[x, count : count + 16, :].astype(jnp.float32)[0:8] for x in range(last)]
    for x in range(1, last - 1):
        base = ocean[x] * lat
        weight[0, x] = base * ocean[x + 1]
        weight[1, x] = base * ocean[x - 1]
        weight[2, x] = jnp.where(lane == ny - 1, 0.0, base * north(ocean[x]))
        weight[3, x] = jnp.where(lane == 0, 0.0, base * south(ocean[x]))
        weight[4, x] = ocean[x]

    @pl.loop(0, count // 16)
    def _(block):
        start = pl.multiple_of(block * 16, 16)
        both = [wide[x, pl.ds(start, 16), :].astype(jnp.float32) for x in range(last)]
        for side in range(2):
            f = [b[side * 8 : side * 8 + 8] for b in both]
            for i, coef in enumerate(PASS_COEFS):
                new = list(f)
                for x in range(i + 1, last - i - 1):
                    centre = f[x]
                    flux = weight[0, x] * (f[x + 1] - centre) + weight[1, x] * (f[x - 1] - centre)
                    flux = flux + weight[2, x] * (north(centre) - centre) + weight[3, x] * (south(centre) - centre)
                    new[x] = centre + coef * flux
                f = new
            for x in range(cols):
                done = weight[4, HALO + x] * f[HALO + x]
                at = pl.multiple_of(x * count + start + side * 8, 8)
                for c in range(y_tiles):
                    spread[c, pl.ds(at, 8), :] = done[:, c * LANES : (c + 1) * LANES]

    for t in range(count // groups):
        for c in range(y_tiles):
            parts = [spread[c, pl.ds(t * groups + g, cols, stride=count), :] for g in range(groups)]
            for g, piece in enumerate(swap_groups(parts, own)):
                packed[c * groups + g, t] = piece.astype(jnp.bfloat16)

    def data_copy(dst, slot):
        return pltpu.make_async_remote_copy(
            src_ref=packed.at[dst],
            dst_ref=land.at[:, pl.ds(pl.multiple_of(slot * cols, cols), cols), :],
            send_sem=data_send.at[dst],
            recv_sem=data_recv.at[slot],
            device_id=(group, dst),
            device_id_type=MESH,
        )

    def each_peer(act):
        def body(step, carry):
            act(peer(step, n))
            return carry

        lax.fori_loop(1, n, body, 0)

    each_peer(lambda dst: data_copy(dst, me).start())
    land[:, pl.ds(pl.multiple_of(me * cols, cols), cols), :] = packed[me]
    reduce_bands()
    each_peer(lambda source: data_copy(source, source).wait_recv())

    for t in range(count // groups):
        turned = land[t].astype(jnp.float32).T
        for c in range(x_tiles):
            stack[c, modes_rows + t * LANES : modes_rows + (t + 1) * LANES, :] = turned[:, c * LANES : (c + 1) * LANES]
    for fy in range(fy_count):
        for c in range(x_tiles):
            at = fy * nx + c * LANES
            rows_ref[modes:total_rows, at : at + LANES] = stack[
                c, pl.ds(modes_rows + fy, total_rows - modes, stride=fy_count), :
            ].astype(jnp.bfloat16)
    late[...] = jnp.zeros_like(late)
    late[:, 0:total_rows] = lax.dot_general(
        rows_ref[modes:total_rows, :], rows_ref[...], (((1,), (1,)), ((), ())), preferred_element_type=jnp.float32
    )

    def late_copy(dst, slot):
        return pltpu.make_async_remote_copy(
            src_ref=late,
            dst_ref=late_land.at[slot],
            send_sem=late_send.at[dst],
            recv_sem=late_recv.at[slot],
            device_id=(group, dst),
            device_id_type=MESH,
        )

    each_peer(lambda dst: late_copy(dst, me).start())
    late_land[me] = late[...]
    finish_bands()
    total_ref[0:modes, :] = gather[...]
    each_peer(lambda source: late_copy(source, source).wait_recv())
    total = late_land[0]
    for slot in range(1, n):
        total = total + late_land[slot]
    total_ref[modes:total_rows, :] = total
    each_peer(lambda dst: late_copy(dst, me).wait_send())
    each_peer(lambda dst: data_copy(dst, me).wait_send())


def solve_kernel(total_cells, nx, gram_ref, weights_ref, rows_ref, basis_ref, coef_ref, k_t, full, out):
    modes = weights_ref.shape[1]
    total_rows = gram_ref.shape[0]
    fy_count = rows_ref.shape[1] // nx
    eye = (
        lax.broadcasted_iota(jnp.int32, (modes, modes), 0) == lax.broadcasted_iota(jnp.int32, (modes, modes), 1)
    )
    full[...] = jnp.zeros_like(full)
    full[0:total_rows, :] = gram_ref[...]
    row = lax.broadcasted_iota(jnp.int32, full.shape, 0)
    column = lax.broadcasted_iota(jnp.int32, full.shape, 1)
    full[...] = jnp.where((row < modes) & (column >= modes), full[...].T, full[...])
    coefficients = full[modes:total_rows, 0:modes] * (1.0 / math.sqrt(total_cells))
    coef_ref[...] = coefficients
    k_t[...] = jnp.zeros_like(k_t)
    k_t[0:modes, 0:modes] = jnp.where(eye, weights_ref[...], 0.0)
    k_t[modes:total_rows, 0:modes] = coefficients.astype(jnp.bfloat16).astype(jnp.float32)
    k = k_t[...].T
    half = jnp.dot(full[...], k_t[...], precision=HIGH, preferred_element_type=jnp.float32)
    gram = jnp.dot(k, half, precision=HIGH, preferred_element_type=jnp.float32)[0:modes, 0:modes] * (1.0 / total_cells)

    a = jnp.concatenate([gram, jnp.where(eye, 1.0, 0.0)], axis=1)
    done = []
    for j in range(modes):
        top = j % 8
        row = a[top : top + 1, :]
        factor = a[:, j : j + 1] * (1.0 / row[:, j : j + 1])
        below = lax.broadcasted_iota(jnp.int32, (a.shape[0], 1), 0) > top
        a = a - jnp.where(below, factor, 0.0) * row
        if top == 7:
            done.append(a[0:8, :])
            a = a[8:, :]
    a = jnp.concatenate(done, axis=0)
    diagonal = jnp.sum(jnp.where(eye, a[:, 0:modes], 0.0), axis=1, keepdims=True)
    inverse = a[:, modes : 2 * modes] * (1.0 / jnp.sqrt(diagonal))
    mix = jnp.dot(inverse, k[0:modes, :], precision=HIGH, preferred_element_type=jnp.float32)[:, 0:total_rows]
    high = mix.astype(jnp.bfloat16)
    low = (mix - high.astype(jnp.float32)).astype(jnp.bfloat16)
    for fy in range(fy_count):
        block = rows_ref[:, fy * nx : (fy + 1) * nx]
        solved = jnp.dot(high, block, preferred_element_type=jnp.float32) + jnp.dot(
            low, block, preferred_element_type=jnp.float32
        )
        for c in range(nx // LANES):
            out[c, pl.ds(fy, modes, stride=fy_count), :] = solved[:, c * LANES : (c + 1) * LANES]
    for c in range(nx // LANES):
        basis_ref[:, c * LANES : (c + 1) * LANES] = out[c].astype(jnp.bfloat16)


def params(limit, collective_id=None):
    if collective_id is None:
        return pltpu.CompilerParams(vmem_limit_bytes=limit)
    return pltpu.CompilerParams(vmem_limit_bytes=limit, collective_id=collective_id, has_side_effects=True)


def local(n, snapshots, basis, mode_weights, land_mask, scale_index, scale_values):
    snaps, fields, cols, ny = snapshots.shape
    modes, _, own, nx = basis.shape
    count = snaps * fields
    fy_count = fields * own
    total_rows = modes + snaps
    total_cells = float(fields * nx * ny)
    limit = 60 * 1024 * 1024
    groups = LANES // own
    bands = modes // 8

    rows, total = pl.pallas_call(
        functools.partial(project_kernel, n, cols),
        out_shape=(
            jax.ShapeDtypeStruct((total_rows, fy_count * nx), jnp.bfloat16),
            jax.ShapeDtypeStruct((total_rows, LANES), jnp.float32),
        ),
        in_specs=[HBM] * 3 + [VMEM] * 2,
        out_specs=(VMEM, VMEM),
        scratch_shapes=[
            pltpu.VMEM((count * cols, ny), jnp.bfloat16),
            pltpu.VMEM((cols, ny), jnp.int32),
            pltpu.VMEM((modes * fy_count, nx), jnp.bfloat16),
            pltpu.VMEM((cols + 2 * HALO, count + 16, ny), jnp.bfloat16),
            pltpu.VMEM((ny // LANES, count * cols, LANES), jnp.float32),
            pltpu.VMEM((5, cols + 2 * HALO, 8, ny), jnp.float32),
            pltpu.VMEM((n, count // groups, cols, LANES), jnp.bfloat16),
            pltpu.VMEM((count // groups, nx, LANES), jnp.bfloat16),
            pltpu.VMEM((nx // LANES, total_rows * fy_count, LANES), jnp.float32),
            pltpu.VMEM((modes, LANES), jnp.float32),
            pltpu.VMEM((n, 8, LANES), jnp.float32),
            pltpu.VMEM((modes, LANES), jnp.float32),
            pltpu.VMEM((snaps, LANES), jnp.float32),
            pltpu.VMEM((n, snaps, LANES), jnp.float32),
        ]
        + [pltpu.SemaphoreType.DMA((k,)) for k in (3, 2, 2, n, n, bands, n, n, bands, n, n)],
        compiler_params=params(limit, 0),
        name="project",
    )(
        snapshots.reshape(count * cols, ny),
        land_mask,
        basis.reshape(modes * fy_count, nx),
        scale_index.reshape(1, ny),
        scale_values.reshape(1, -1),
    )
    new_basis, coefficients = pl.pallas_call(
        functools.partial(solve_kernel, total_cells, nx),
        out_shape=(
            jax.ShapeDtypeStruct((modes * fy_count, nx), jnp.bfloat16),
            jax.ShapeDtypeStruct((snaps, modes), jnp.float32),
        ),
        in_specs=[VMEM] * 3,
        out_specs=(VMEM, VMEM),
        scratch_shapes=[
            pltpu.VMEM((LANES, LANES), jnp.float32),
            pltpu.VMEM((LANES, LANES), jnp.float32),
            pltpu.VMEM((nx // LANES, modes * fy_count, LANES), jnp.float32),
        ],
        compiler_params=params(limit),
        name="solve",
    )(total, mode_weights.reshape(1, modes), rows)
    return new_basis.reshape(basis.shape), coefficients


def solution(mesh):
    placed = (
        P("group", None, "space", None),
        P("group", None, "space", None),
        P("group"),
        P("space", None),
        P(),
        P(),
    )
    return jax.shard_map(
        functools.partial(local, mesh.shape["space"]),
        mesh=mesh,
        in_specs=placed,
        out_specs=(P("group", None, "space", None), P("group", None)),
        check_vma=False,
    )
```

```python
import functools
import math

import jax
import jax.numpy as jnp
from jax import lax
from jax.experimental import pallas as pl
from jax.experimental.pallas import tpu as pltpu
from jax.sharding import PartitionSpec as P

PASS_COEFS = (1.0, 0.95, 0.85, 0.7, 0.5, 0.3)
HALO = len(PASS_COEFS)
LANES = 128
HIGH = lax.Precision.HIGHEST
MESH = pl.DeviceIdType.MESH
VMEM = pl.BlockSpec(memory_space=pltpu.VMEM)
HBM = pl.BlockSpec(memory_space=pltpu.HBM)


def peer(step, n):
    return lax.rem(lax.axis_index("space") + step, n)


def greet(n):
    group = lax.axis_index("group")
    barrier = pltpu.get_barrier_semaphore()

    def signal(step, carry):
        pl.semaphore_signal(barrier, inc=1, device_id=(group, peer(step, n)), device_id_type=MESH)
        return carry

    lax.fori_loop(1, n, signal, 0)
    return barrier


def band_sum(n, bands, part_ref, land, gather, send_part, recv_part, send_sum, recv_sum):
    me = lax.axis_index("space")
    group = lax.axis_index("group")
    mine = lax.div(me * bands + n - 1, n)

    def owner(band):
        return lax.div(band * n, bands)

    def band_rows(band):
        return pl.ds(pl.multiple_of(band * 8, 8), 8)

    def part_copy(band, slot):
        return pltpu.make_async_remote_copy(
            src_ref=part_ref.at[band_rows(band)],
            dst_ref=land.at[slot],
            send_sem=send_part.at[band],
            recv_sem=recv_part.at[slot],
            device_id=(group, owner(band)),
            device_id_type=MESH,
        )

    def sum_copy(band, dst):
        return pltpu.make_async_remote_copy(
            src_ref=gather.at[band_rows(band)],
            dst_ref=gather.at[band_rows(band)],
            send_sem=send_sum.at[dst],
            recv_sem=recv_sum.at[band],
            device_id=(group, dst),
            device_id_type=MESH,
        )

    def others(act):
        def body(band, carry):
            @pl.when(owner(band) != me)
            def _():
                act(band)

            return carry

        lax.fori_loop(0, bands, body, 0)

    def peers(act):
        def body(step, carry):
            act(peer(step, n))
            return carry

        lax.fori_loop(1, n, body, 0)

    owns = (mine < bands) & (owner(mine) == me)

    def start():
        others(lambda band: part_copy(band, me).start())

    def reduce():
        @pl.when(owns)
        def _():
            land[me] = part_ref[band_rows(mine)]
            peers(lambda source: part_copy(mine, source).wait_recv())
            total = land[0]
            for slot in range(1, n):
                total = total + land[slot]
            gather[band_rows(mine), :] = total
            peers(lambda dst: sum_copy(mine, dst).start())

    def finish():
        others(lambda band: sum_copy(band, me).wait_recv())
        others(lambda band: part_copy(band, me).wait_send())

        @pl.when(owns)
        def _():
            peers(lambda dst: sum_copy(mine, dst).wait_send())

    return start, reduce, finish


def swap_groups(parts, width):
    parts = list(parts)
    size = parts[0].shape[1]
    lane = lax.broadcasted_iota(jnp.int32, parts[0].shape, 1)
    bit = 1
    while bit < len(parts):
        shift = bit * width
        upper = lax.rem(lax.div(lane, shift), 2) == 1
        for s in range(len(parts)):
            if not s & bit:
                a, b = parts[s], parts[s | bit]
                parts[s] = jnp.where(upper, pltpu.roll(b, shift, 1), a)
                parts[s | bit] = jnp.where(upper, b, pltpu.roll(a, size - shift, 1))
        bit *= 2
    return parts


def project_kernel(
    n,
    cols,
    snaps_hbm,
    mask_hbm,
    basis_hbm,
    index_ref,
    values_ref,
    rows_ref,
    total_ref,
    snaps_ref,
    mask_ref,
    basis_ref,
    wide,
    spread,
    weight,
    packed,
    land,
    stack,
    part,
    band_land,
    gather,
    late,
    late_land,
    loaded,
    edge_send,
    edge_recv,
    data_send,
    data_recv,
    send_part,
    recv_part,
    send_sum,
    recv_sum,
    late_send,
    late_recv,
):
    me = lax.axis_index("space")
    group = lax.axis_index("group")
    loads = [
        pltpu.make_async_copy(src, dst, loaded.at[i])
        for i, (src, dst) in enumerate(((snaps_hbm, snaps_ref), (mask_hbm, mask_ref), (basis_hbm, basis_ref)))
    ]
    for load in loads:
        load.start()
    barrier = greet(n)
    count = snaps_ref.shape[0] // cols
    ny, nx = snaps_ref.shape[1], basis_ref.shape[1]
    own = ny // n
    groups = LANES // own
    modes_rows = basis_ref.shape[0]
    total_rows, fy_count = rows_ref.shape[0], rows_ref.shape[1] // nx
    modes = modes_rows // fy_count
    y_tiles, x_tiles = ny // LANES, nx // LANES

    loads[0].wait()
    loads[1].wait()
    for c in range(y_tiles):
        spread[c] = snaps_ref[:, c * LANES : (c + 1) * LANES].astype(jnp.float32)
    for x in range(cols):
        for c in range(y_tiles):
            wide[HALO + x, 0:count, c * LANES : (c + 1) * LANES] = spread[
                c, pl.ds(x, count, stride=cols), :
            ].astype(jnp.bfloat16)
        line = mask_ref[x : x + 1, :].astype(jnp.float32)
        wide[HALO + x, count : count + 16, :] = jnp.broadcast_to(line, (16, ny)).astype(jnp.bfloat16)

    pl.semaphore_wait(barrier, n - 1)

    def edge_copy(first, to, where, who):
        return pltpu.make_async_remote_copy(
            src_ref=wide.at[pl.ds(first, HALO)],
            dst_ref=wide.at[pl.ds(to, HALO)],
            send_sem=edge_send.at[where],
            recv_sem=edge_recv.at[where],
            device_id=(group, who),
            device_id_type=MESH,
        )

    to_left = edge_copy(HALO, HALO + cols, 0, peer(n - 1, n))
    to_right = edge_copy(cols, 0, 1, peer(1, n))
    to_left.start()
    to_right.start()

    loads[2].wait()
    for c in range(x_tiles):
        stack[c, 0:modes_rows, :] = basis_ref[:, c * LANES : (c + 1) * LANES].astype(jnp.float32)
    for fy in range(fy_count):
        for c in range(x_tiles):
            at = fy * nx + c * LANES
            rows_ref[0:modes, at : at + LANES] = stack[c, pl.ds(fy, modes, stride=fy_count), :].astype(jnp.bfloat16)
    part[...] = jnp.zeros_like(part)
    part[0:modes, 0:modes] = lax.dot_general(
        rows_ref[0:modes, :], rows_ref[0:modes, :], (((1,), (1,)), ((), ())), preferred_element_type=jnp.float32
    )
    start_bands, reduce_bands, finish_bands = band_sum(
        n, modes // 8, part, band_land, gather, send_part, recv_part, send_sum, recv_sum
    )
    start_bands()
    lat = jnp.zeros((1, ny), jnp.float32)
    for level in range(values_ref.shape[1]):
        lat = lat + jnp.where(index_ref[...] == level, values_ref[0:1, level : level + 1], 0.0)
    lane = lax.broadcasted_iota(jnp.int32, (8, ny), 1)

    to_left.wait()
    to_right.wait()

    def north(a):
        return pltpu.roll(a, ny - 1, 1)

    def south(a):
        return pltpu.roll(a, 1, 1)

    last = cols + 2 * HALO
    ocean = [wide[x, count : count + 16, :].astype(jnp.float32)[0:8] for x in range(last)]
    for x in range(1, last - 1):
        base = ocean[x] * lat
        weight[0, x] = base * ocean[x + 1]
        weight[1, x] = base * ocean[x - 1]
        weight[2, x] = jnp.where(lane == ny - 1, 0.0, base * north(ocean[x]))
        weight[3, x] = jnp.where(lane == 0, 0.0, base * south(ocean[x]))
        weight[4, x] = ocean[x]

    @pl.loop(0, count // 16)
    def _(block):
        start = pl.multiple_of(block * 16, 16)
        both = [wide[x, pl.ds(start, 16), :].astype(jnp.float32) for x in range(last)]
        for side in range(2):
            f = [b[side * 8 : side * 8 + 8] for b in both]
            for i, coef in enumerate(PASS_COEFS):
                new = list(f)
                for x in range(i + 1, last - i - 1):
                    centre = f[x]
                    flux = weight[0, x] * (f[x + 1] - centre) + weight[1, x] * (f[x - 1] - centre)
                    flux = flux + weight[2, x] * (north(centre) - centre) + weight[3, x] * (south(centre) - centre)
                    new[x] = centre + coef * flux
                f = new
            for x in range(cols):
                done = weight[4, HALO + x] * f[HALO + x]
                at = pl.multiple_of(x * count + start + side * 8, 8)
                for c in range(y_tiles):
                    spread[c, pl.ds(at, 8), :] = done[:, c * LANES : (c + 1) * LANES]

    for t in range(count // groups):
        for c in range(y_tiles):
            parts = [spread[c, pl.ds(t * groups + g, cols, stride=count), :] for g in range(groups)]
            for g, piece in enumerate(swap_groups(parts, own)):
                packed[c * groups + g, t] = piece.astype(jnp.bfloat16)

    def data_copy(dst, slot):
        return pltpu.make_async_remote_copy(
            src_ref=packed.at[dst],
            dst_ref=land.at[:, pl.ds(pl.multiple_of(slot * cols, cols), cols), :],
            send_sem=data_send.at[dst],
            recv_sem=data_recv.at[slot],
            device_id=(group, dst),
            device_id_type=MESH,
        )

    def each_peer(act):
        def body(step, carry):
            act(peer(step, n))
            return carry

        lax.fori_loop(1, n, body, 0)

    each_peer(lambda dst: data_copy(dst, me).start())
    land[:, pl.ds(pl.multiple_of(me * cols, cols), cols), :] = packed[me]
    reduce_bands()
    each_peer(lambda source: data_copy(source, source).wait_recv())

    for t in range(count // groups):
        turned = land[t].astype(jnp.float32).T
        for c in range(x_tiles):
            stack[c, modes_rows + t * LANES : modes_rows + (t + 1) * LANES, :] = turned[:, c * LANES : (c + 1) * LANES]
    for fy in range(fy_count):
        for c in range(x_tiles):
            at = fy * nx + c * LANES
            rows_ref[modes:total_rows, at : at + LANES] = stack[
                c, pl.ds(modes_rows + fy, total_rows - modes, stride=fy_count), :
            ].astype(jnp.bfloat16)
    late[...] = jnp.zeros_like(late)
    late[:, 0:total_rows] = lax.dot_general(
        rows_ref[modes:total_rows, :], rows_ref[...], (((1,), (1,)), ((), ())), preferred_element_type=jnp.float32
    )

    def late_copy(dst, slot):
        return pltpu.make_async_remote_copy(
            src_ref=late,
            dst_ref=late_land.at[slot],
            send_sem=late_send.at[dst],
            recv_sem=late_recv.at[slot],
            device_id=(group, dst),
            device_id_type=MESH,
        )

    each_peer(lambda dst: late_copy(dst, me).start())
    late_land[me] = late[...]
    finish_bands()
    total_ref[0:modes, :] = gather[...]
    each_peer(lambda source: late_copy(source, source).wait_recv())
    total = late_land[0]
    for slot in range(1, n):
        total = total + late_land[slot]
    total_ref[modes:total_rows, :] = total
    each_peer(lambda dst: late_copy(dst, me).wait_send())
    each_peer(lambda dst: data_copy(dst, me).wait_send())


def solve_kernel(total_cells, nx, gram_ref, weights_ref, rows_ref, basis_ref, coef_ref, k_t, full, out):
    modes = weights_ref.shape[1]
    total_rows = gram_ref.shape[0]
    fy_count = rows_ref.shape[1] // nx
    eye = (
        lax.broadcasted_iota(jnp.int32, (modes, modes), 0) == lax.broadcasted_iota(jnp.int32, (modes, modes), 1)
    )
    full[...] = jnp.zeros_like(full)
    full[0:total_rows, :] = gram_ref[...]
    row = lax.broadcasted_iota(jnp.int32, full.shape, 0)
    column = lax.broadcasted_iota(jnp.int32, full.shape, 1)
    full[...] = jnp.where((row < modes) & (column >= modes), full[...].T, full[...])
    coefficients = full[modes:total_rows, 0:modes] * (1.0 / math.sqrt(total_cells))
    coef_ref[...] = coefficients
    k_t[...] = jnp.zeros_like(k_t)
    k_t[0:modes, 0:modes] = jnp.where(eye, weights_ref[...], 0.0)
    k_t[modes:total_rows, 0:modes] = coefficients.astype(jnp.bfloat16).astype(jnp.float32)
    k = k_t[...].T
    half = jnp.dot(full[...], k_t[...], precision=HIGH, preferred_element_type=jnp.float32)
    gram = jnp.dot(k, half, precision=HIGH, preferred_element_type=jnp.float32)[0:modes, 0:modes] * (1.0 / total_cells)

    a = jnp.concatenate([gram, jnp.where(eye, 1.0, 0.0)], axis=1)
    done = []
    for j in range(0, modes, 2):
        top = j % 8
        first, second = a[top : top + 1, :], a[top + 1 : top + 2, :]
        column, beside = a[:, j : j + 1], a[:, j + 1 : j + 2]
        inv_first = 1.0 / first[:, j : j + 1]
        across = first[:, j + 1 : j + 2]
        scale = second[:, j : j + 1] * inv_first
        inv_second = 1.0 / (second[:, j + 1 : j + 2] - scale * across)
        factor = column * inv_first
        factor_next = (beside - factor * across) * inv_second
        second = second - scale * first
        row_at = lax.broadcasted_iota(jnp.int32, (a.shape[0], 1), 0)
        a = a - jnp.where(row_at > top, factor, 0.0) * first - jnp.where(row_at > top + 1, factor_next, 0.0) * second
        if top == 6:
            done.append(a[0:8, :])
            a = a[8:, :]
    a = jnp.concatenate(done, axis=0)
    diagonal = jnp.sum(jnp.where(eye, a[:, 0:modes], 0.0), axis=1, keepdims=True)
    inverse = a[:, modes : 2 * modes] * (1.0 / jnp.sqrt(diagonal))
    mix = jnp.dot(inverse, k[0:modes, :], precision=HIGH, preferred_element_type=jnp.float32)[:, 0:total_rows]
    high = mix.astype(jnp.bfloat16)
    low = (mix - high.astype(jnp.float32)).astype(jnp.bfloat16)
    for fy in range(fy_count):
        block = rows_ref[:, fy * nx : (fy + 1) * nx]
        solved = jnp.dot(high, block, preferred_element_type=jnp.float32) + jnp.dot(
            low, block, preferred_element_type=jnp.float32
        )
        for c in range(nx // LANES):
            out[c, pl.ds(fy, modes, stride=fy_count), :] = solved[:, c * LANES : (c + 1) * LANES]
    for c in range(nx // LANES):
        basis_ref[:, c * LANES : (c + 1) * LANES] = out[c].astype(jnp.bfloat16)


def params(limit, collective_id=None):
    if collective_id is None:
        return pltpu.CompilerParams(vmem_limit_bytes=limit)
    return pltpu.CompilerParams(vmem_limit_bytes=limit, collective_id=collective_id, has_side_effects=True)


def local(n, snapshots, basis, mode_weights, land_mask, scale_index, scale_values):
    snaps, fields, cols, ny = snapshots.shape
    modes, _, own, nx = basis.shape
    count = snaps * fields
    fy_count = fields * own
    total_rows = modes + snaps
    total_cells = float(fields * nx * ny)
    limit = 60 * 1024 * 1024
    groups = LANES // own
    bands = modes // 8

    rows, total = pl.pallas_call(
        functools.partial(project_kernel, n, cols),
        out_shape=(
            jax.ShapeDtypeStruct((total_rows, fy_count * nx), jnp.bfloat16),
            jax.ShapeDtypeStruct((total_rows, LANES), jnp.float32),
        ),
        in_specs=[HBM] * 3 + [VMEM] * 2,
        out_specs=(VMEM, VMEM),
        scratch_shapes=[
            pltpu.VMEM((count * cols, ny), jnp.bfloat16),
            pltpu.VMEM((cols, ny), jnp.int32),
            pltpu.VMEM((modes * fy_count, nx), jnp.bfloat16),
            pltpu.VMEM((cols + 2 * HALO, count + 16, ny), jnp.bfloat16),
            pltpu.VMEM((ny // LANES, count * cols, LANES), jnp.float32),
            pltpu.VMEM((5, cols + 2 * HALO, 8, ny), jnp.float32),
            pltpu.VMEM((n, count // groups, cols, LANES), jnp.bfloat16),
            pltpu.VMEM((count // groups, nx, LANES), jnp.bfloat16),
            pltpu.VMEM((nx // LANES, total_rows * fy_count, LANES), jnp.float32),
            pltpu.VMEM((modes, LANES), jnp.float32),
            pltpu.VMEM((n, 8, LANES), jnp.float32),
            pltpu.VMEM((modes, LANES), jnp.float32),
            pltpu.VMEM((snaps, LANES), jnp.float32),
            pltpu.VMEM((n, snaps, LANES), jnp.float32),
        ]
        + [pltpu.SemaphoreType.DMA((k,)) for k in (3, 2, 2, n, n, bands, n, n, bands, n, n)],
        compiler_params=params(limit, 0),
        name="project",
    )(
        snapshots.reshape(count * cols, ny),
        land_mask,
        basis.reshape(modes * fy_count, nx),
        scale_index.reshape(1, ny),
        scale_values.reshape(1, -1),
    )
    new_basis, coefficients = pl.pallas_call(
        functools.partial(solve_kernel, total_cells, nx),
        out_shape=(
            jax.ShapeDtypeStruct((modes * fy_count, nx), jnp.bfloat16),
            jax.ShapeDtypeStruct((snaps, modes), jnp.float32),
        ),
        in_specs=[VMEM] * 3,
        out_specs=(VMEM, VMEM),
        scratch_shapes=[
            pltpu.VMEM((LANES, LANES), jnp.float32),
            pltpu.VMEM((LANES, LANES), jnp.float32),
            pltpu.VMEM((nx // LANES, modes * fy_count, LANES), jnp.float32),
        ],
        compiler_params=params(limit),
        name="solve",
    )(total, mode_weights.reshape(1, modes), rows)
    return new_basis.reshape(basis.shape), coefficients


def solution(mesh):
    placed = (
        P("group", None, "space", None),
        P("group", None, "space", None),
        P("group"),
        P("space", None),
        P(),
        P(),
    )
    return jax.shard_map(
        functools.partial(local, mesh.shape["space"]),
        mesh=mesh,
        in_specs=placed,
        out_specs=(P("group", None, "space", None), P("group", None)),
        check_vma=False,
    )
```

```python
import functools
import math

import jax
import jax.numpy as jnp
from jax import lax
from jax.experimental import pallas as pl
from jax.experimental.pallas import tpu as pltpu
from jax.sharding import PartitionSpec as P

PASS_COEFS = (1.0, 0.95, 0.85, 0.7, 0.5, 0.3)
HALO = len(PASS_COEFS)
LANES = 128
HIGH = lax.Precision.HIGHEST
MESH = pl.DeviceIdType.MESH
VMEM = pl.BlockSpec(memory_space=pltpu.VMEM)
HBM = pl.BlockSpec(memory_space=pltpu.HBM)


def peer(step, n):
    return lax.rem(lax.axis_index("space") + step, n)


def greet(n):
    group = lax.axis_index("group")
    barrier = pltpu.get_barrier_semaphore()

    def signal(step, carry):
        pl.semaphore_signal(barrier, inc=1, device_id=(group, peer(step, n)), device_id_type=MESH)
        return carry

    lax.fori_loop(1, n, signal, 0)
    return barrier


def band_sum(n, bands, part_ref, land, gather, send_part, recv_part, send_sum, recv_sum):
    me = lax.axis_index("space")
    group = lax.axis_index("group")
    mine = lax.div(me * bands + n - 1, n)

    def owner(band):
        return lax.div(band * n, bands)

    def band_rows(band):
        return pl.ds(pl.multiple_of(band * 8, 8), 8)

    def part_copy(band, slot):
        return pltpu.make_async_remote_copy(
            src_ref=part_ref.at[band_rows(band)],
            dst_ref=land.at[slot],
            send_sem=send_part.at[band],
            recv_sem=recv_part.at[slot],
            device_id=(group, owner(band)),
            device_id_type=MESH,
        )

    def sum_copy(band, dst):
        return pltpu.make_async_remote_copy(
            src_ref=gather.at[band_rows(band)],
            dst_ref=gather.at[band_rows(band)],
            send_sem=send_sum.at[dst],
            recv_sem=recv_sum.at[band],
            device_id=(group, dst),
            device_id_type=MESH,
        )

    def others(act):
        def body(band, carry):
            @pl.when(owner(band) != me)
            def _():
                act(band)

            return carry

        lax.fori_loop(0, bands, body, 0)

    def peers(act):
        def body(step, carry):
            act(peer(step, n))
            return carry

        lax.fori_loop(1, n, body, 0)

    owns = (mine < bands) & (owner(mine) == me)

    def start():
        others(lambda band: part_copy(band, me).start())

    def reduce():
        @pl.when(owns)
        def _():
            land[me] = part_ref[band_rows(mine)]
            peers(lambda source: part_copy(mine, source).wait_recv())
            total = land[0]
            for slot in range(1, n):
                total = total + land[slot]
            gather[band_rows(mine), :] = total
            peers(lambda dst: sum_copy(mine, dst).start())

    def finish():
        others(lambda band: sum_copy(band, me).wait_recv())
        others(lambda band: part_copy(band, me).wait_send())

        @pl.when(owns)
        def _():
            peers(lambda dst: sum_copy(mine, dst).wait_send())

    return start, reduce, finish


def swap_groups(parts, width):
    parts = list(parts)
    size = parts[0].shape[1]
    lane = lax.broadcasted_iota(jnp.int32, parts[0].shape, 1)
    bit = 1
    while bit < len(parts):
        shift = bit * width
        upper = lax.rem(lax.div(lane, shift), 2) == 1
        for s in range(len(parts)):
            if not s & bit:
                a, b = parts[s], parts[s | bit]
                parts[s] = jnp.where(upper, pltpu.roll(b, shift, 1), a)
                parts[s | bit] = jnp.where(upper, b, pltpu.roll(a, size - shift, 1))
        bit *= 2
    return parts


def project_kernel(
    n,
    cols,
    snaps_hbm,
    mask_hbm,
    basis_hbm,
    index_ref,
    values_ref,
    rows_ref,
    total_ref,
    snaps_ref,
    mask_ref,
    basis_ref,
    wide,
    spread,
    weight,
    packed,
    land,
    stack,
    part,
    band_land,
    gather,
    late,
    late_land,
    loaded,
    edge_send,
    edge_recv,
    data_send,
    data_recv,
    send_part,
    recv_part,
    send_sum,
    recv_sum,
    late_send,
    late_recv,
):
    me = lax.axis_index("space")
    group = lax.axis_index("group")
    loads = [
        pltpu.make_async_copy(src, dst, loaded.at[i])
        for i, (src, dst) in enumerate(((snaps_hbm, snaps_ref), (mask_hbm, mask_ref), (basis_hbm, basis_ref)))
    ]
    for load in loads:
        load.start()
    barrier = greet(n)
    count = snaps_ref.shape[0] // cols
    ny, nx = snaps_ref.shape[1], basis_ref.shape[1]
    own = ny // n
    groups = LANES // own
    modes_rows = basis_ref.shape[0]
    total_rows, fy_count = rows_ref.shape[0], rows_ref.shape[1] // nx
    modes = modes_rows // fy_count
    y_tiles, x_tiles = ny // LANES, nx // LANES

    loads[0].wait()
    loads[1].wait()
    for c in range(y_tiles):
        spread[c] = snaps_ref[:, c * LANES : (c + 1) * LANES].astype(jnp.float32)
    for x in range(cols):
        for c in range(y_tiles):
            wide[HALO + x, 0:count, c * LANES : (c + 1) * LANES] = spread[
                c, pl.ds(x, count, stride=cols), :
            ].astype(jnp.bfloat16)
        line = mask_ref[x : x + 1, :].astype(jnp.float32)
        wide[HALO + x, count : count + 16, :] = jnp.broadcast_to(line, (16, ny)).astype(jnp.bfloat16)

    pl.semaphore_wait(barrier, n - 1)

    def edge_copy(first, to, where, who):
        return pltpu.make_async_remote_copy(
            src_ref=wide.at[pl.ds(first, HALO)],
            dst_ref=wide.at[pl.ds(to, HALO)],
            send_sem=edge_send.at[where],
            recv_sem=edge_recv.at[where],
            device_id=(group, who),
            device_id_type=MESH,
        )

    to_left = edge_copy(HALO, HALO + cols, 0, peer(n - 1, n))
    to_right = edge_copy(cols, 0, 1, peer(1, n))
    to_left.start()
    to_right.start()

    loads[2].wait()
    for c in range(x_tiles):
        stack[c, 0:modes_rows, :] = basis_ref[:, c * LANES : (c + 1) * LANES].astype(jnp.float32)
    for fy in range(fy_count):
        for c in range(x_tiles):
            at = fy * nx + c * LANES
            rows_ref[0:modes, at : at + LANES] = stack[c, pl.ds(fy, modes, stride=fy_count), :].astype(jnp.bfloat16)
    part[...] = jnp.zeros_like(part)
    part[0:modes, 0:modes] = lax.dot_general(
        rows_ref[0:modes, :], rows_ref[0:modes, :], (((1,), (1,)), ((), ())), preferred_element_type=jnp.float32
    )
    start_bands, reduce_bands, finish_bands = band_sum(
        n, modes // 8, part, band_land, gather, send_part, recv_part, send_sum, recv_sum
    )
    start_bands()
    lat = jnp.zeros((1, ny), jnp.float32)
    for level in range(values_ref.shape[1]):
        lat = lat + jnp.where(index_ref[...] == level, values_ref[0:1, level : level + 1], 0.0)
    lane = lax.broadcasted_iota(jnp.int32, (8, ny), 1)

    to_left.wait()
    to_right.wait()

    def north(a):
        return pltpu.roll(a, ny - 1, 1)

    def south(a):
        return pltpu.roll(a, 1, 1)

    last = cols + 2 * HALO
    ocean = [wide[x, count : count + 16, :].astype(jnp.float32)[0:8] for x in range(last)]
    for x in range(1, last - 1):
        base = ocean[x] * lat
        weight[0, x] = base * ocean[x + 1]
        weight[1, x] = base * ocean[x - 1]
        weight[2, x] = jnp.where(lane == ny - 1, 0.0, base * north(ocean[x]))
        weight[3, x] = jnp.where(lane == 0, 0.0, base * south(ocean[x]))
        weight[4, x] = ocean[x]

    @pl.loop(0, count // 16)
    def _(block):
        start = pl.multiple_of(block * 16, 16)
        both = [wide[x, pl.ds(start, 16), :].astype(jnp.float32) for x in range(last)]
        for side in range(2):
            f = [b[side * 8 : side * 8 + 8] for b in both]
            for i, coef in enumerate(PASS_COEFS):
                new = list(f)
                for x in range(i + 1, last - i - 1):
                    centre = f[x]
                    flux = weight[0, x] * (f[x + 1] - centre) + weight[1, x] * (f[x - 1] - centre)
                    flux = flux + weight[2, x] * (north(centre) - centre) + weight[3, x] * (south(centre) - centre)
                    new[x] = centre + coef * flux
                f = new
            for x in range(cols):
                done = weight[4, HALO + x] * f[HALO + x]
                at = pl.multiple_of(x * count + start + side * 8, 8)
                for c in range(y_tiles):
                    spread[c, pl.ds(at, 8), :] = done[:, c * LANES : (c + 1) * LANES]

    for t in range(count // groups):
        for c in range(y_tiles):
            parts = [spread[c, pl.ds(t * groups + g, cols, stride=count), :] for g in range(groups)]
            for g, piece in enumerate(swap_groups(parts, own)):
                packed[c * groups + g, t] = piece.astype(jnp.bfloat16)

    def data_copy(dst, slot):
        return pltpu.make_async_remote_copy(
            src_ref=packed.at[dst],
            dst_ref=land.at[:, pl.ds(pl.multiple_of(slot * cols, cols), cols), :],
            send_sem=data_send.at[dst],
            recv_sem=data_recv.at[slot],
            device_id=(group, dst),
            device_id_type=MESH,
        )

    def each_peer(act):
        def body(step, carry):
            act(peer(step, n))
            return carry

        lax.fori_loop(1, n, body, 0)

    each_peer(lambda dst: data_copy(dst, me).start())
    land[:, pl.ds(pl.multiple_of(me * cols, cols), cols), :] = packed[me]
    reduce_bands()
    each_peer(lambda source: data_copy(source, source).wait_recv())

    for t in range(count // groups):
        turned = land[t].astype(jnp.float32).T
        for c in range(x_tiles):
            stack[c, modes_rows + t * LANES : modes_rows + (t + 1) * LANES, :] = turned[:, c * LANES : (c + 1) * LANES]
    for fy in range(fy_count):
        for c in range(x_tiles):
            at = fy * nx + c * LANES
            rows_ref[modes:total_rows, at : at + LANES] = stack[
                c, pl.ds(modes_rows + fy, total_rows - modes, stride=fy_count), :
            ].astype(jnp.bfloat16)
    late[...] = jnp.zeros_like(late)
    late[:, 0:total_rows] = lax.dot_general(
        rows_ref[modes:total_rows, :], rows_ref[...], (((1,), (1,)), ((), ())), preferred_element_type=jnp.float32
    )

    def late_copy(dst, slot):
        return pltpu.make_async_remote_copy(
            src_ref=late,
            dst_ref=late_land.at[slot],
            send_sem=late_send.at[dst],
            recv_sem=late_recv.at[slot],
            device_id=(group, dst),
            device_id_type=MESH,
        )

    each_peer(lambda dst: late_copy(dst, me).start())
    late_land[me] = late[...]
    finish_bands()
    total_ref[0:modes, :] = gather[...]
    each_peer(lambda source: late_copy(source, source).wait_recv())
    total = late_land[0]
    for slot in range(1, n):
        total = total + late_land[slot]
    total_ref[modes:total_rows, :] = total
    each_peer(lambda dst: late_copy(dst, me).wait_send())
    each_peer(lambda dst: data_copy(dst, me).wait_send())


def solve_kernel(total_cells, nx, gram_ref, weights_ref, rows_ref, basis_ref, coef_ref, k_t, full, out):
    modes = weights_ref.shape[1]
    total_rows = gram_ref.shape[0]
    fy_count = rows_ref.shape[1] // nx
    eye = (
        lax.broadcasted_iota(jnp.int32, (modes, modes), 0) == lax.broadcasted_iota(jnp.int32, (modes, modes), 1)
    )
    full[...] = jnp.zeros_like(full)
    full[0:total_rows, :] = gram_ref[...]
    row = lax.broadcasted_iota(jnp.int32, full.shape, 0)
    column = lax.broadcasted_iota(jnp.int32, full.shape, 1)
    full[...] = jnp.where((row < modes) & (column >= modes), full[...].T, full[...])
    coefficients = full[modes:total_rows, 0:modes] * (1.0 / math.sqrt(total_cells))
    coef_ref[...] = coefficients
    k_t[...] = jnp.zeros_like(k_t)
    k_t[0:modes, 0:modes] = jnp.where(eye, weights_ref[...], 0.0)
    k_t[modes:total_rows, 0:modes] = coefficients.astype(jnp.bfloat16).astype(jnp.float32)
    k = k_t[...].T
    half = jnp.dot(full[...], k_t[...], precision=HIGH, preferred_element_type=jnp.float32)
    gram = jnp.dot(k, half, precision=HIGH, preferred_element_type=jnp.float32)[0:modes, 0:modes] * (1.0 / total_cells)

    a = jnp.concatenate([gram, jnp.where(eye, 1.0, 0.0)], axis=1)
    done = []
    for j in range(modes):
        top = j % 8
        row = a[top : top + 1, :]
        scaled = row * (1.0 / row[:, j : j + 1])
        below = lax.broadcasted_iota(jnp.int32, (a.shape[0], 1), 0) > top
        a = a - jnp.where(below, a[:, j : j + 1], 0.0) * scaled
        if top == 7:
            done.append(a[0:8, :])
            a = a[8:, :]
    a = jnp.concatenate(done, axis=0)
    diagonal = jnp.sum(jnp.where(eye, a[:, 0:modes], 0.0), axis=1, keepdims=True)
    inverse = a[:, modes : 2 * modes] * (1.0 / jnp.sqrt(diagonal))
    mix = jnp.dot(inverse, k[0:modes, :], precision=HIGH, preferred_element_type=jnp.float32)[:, 0:total_rows]
    high = mix.astype(jnp.bfloat16)
    low = (mix - high.astype(jnp.float32)).astype(jnp.bfloat16)
    for fy in range(fy_count):
        block = rows_ref[:, fy * nx : (fy + 1) * nx]
        solved = jnp.dot(high, block, preferred_element_type=jnp.float32) + jnp.dot(
            low, block, preferred_element_type=jnp.float32
        )
        for c in range(nx // LANES):
            out[c, pl.ds(fy, modes, stride=fy_count), :] = solved[:, c * LANES : (c + 1) * LANES]
    for c in range(nx // LANES):
        basis_ref[:, c * LANES : (c + 1) * LANES] = out[c].astype(jnp.bfloat16)


def params(limit, collective_id=None):
    if collective_id is None:
        return pltpu.CompilerParams(vmem_limit_bytes=limit)
    return pltpu.CompilerParams(vmem_limit_bytes=limit, collective_id=collective_id, has_side_effects=True)


def local(n, snapshots, basis, mode_weights, land_mask, scale_index, scale_values):
    snaps, fields, cols, ny = snapshots.shape
    modes, _, own, nx = basis.shape
    count = snaps * fields
    fy_count = fields * own
    total_rows = modes + snaps
    total_cells = float(fields * nx * ny)
    limit = 60 * 1024 * 1024
    groups = LANES // own
    bands = modes // 8

    rows, total = pl.pallas_call(
        functools.partial(project_kernel, n, cols),
        out_shape=(
            jax.ShapeDtypeStruct((total_rows, fy_count * nx), jnp.bfloat16),
            jax.ShapeDtypeStruct((total_rows, LANES), jnp.float32),
        ),
        in_specs=[HBM] * 3 + [VMEM] * 2,
        out_specs=(VMEM, VMEM),
        scratch_shapes=[
            pltpu.VMEM((count * cols, ny), jnp.bfloat16),
            pltpu.VMEM((cols, ny), jnp.int32),
            pltpu.VMEM((modes * fy_count, nx), jnp.bfloat16),
            pltpu.VMEM((cols + 2 * HALO, count + 16, ny), jnp.bfloat16),
            pltpu.VMEM((ny // LANES, count * cols, LANES), jnp.float32),
            pltpu.VMEM((5, cols + 2 * HALO, 8, ny), jnp.float32),
            pltpu.VMEM((n, count // groups, cols, LANES), jnp.bfloat16),
            pltpu.VMEM((count // groups, nx, LANES), jnp.bfloat16),
            pltpu.VMEM((nx // LANES, total_rows * fy_count, LANES), jnp.float32),
            pltpu.VMEM((modes, LANES), jnp.float32),
            pltpu.VMEM((n, 8, LANES), jnp.float32),
            pltpu.VMEM((modes, LANES), jnp.float32),
            pltpu.VMEM((snaps, LANES), jnp.float32),
            pltpu.VMEM((n, snaps, LANES), jnp.float32),
        ]
        + [pltpu.SemaphoreType.DMA((k,)) for k in (3, 2, 2, n, n, bands, n, n, bands, n, n)],
        compiler_params=params(limit, 0),
        name="project",
    )(
        snapshots.reshape(count * cols, ny),
        land_mask,
        basis.reshape(modes * fy_count, nx),
        scale_index.reshape(1, ny),
        scale_values.reshape(1, -1),
    )
    new_basis, coefficients = pl.pallas_call(
        functools.partial(solve_kernel, total_cells, nx),
        out_shape=(
            jax.ShapeDtypeStruct((modes * fy_count, nx), jnp.bfloat16),
            jax.ShapeDtypeStruct((snaps, modes), jnp.float32),
        ),
        in_specs=[VMEM] * 3,
        out_specs=(VMEM, VMEM),
        scratch_shapes=[
            pltpu.VMEM((LANES, LANES), jnp.float32),
            pltpu.VMEM((LANES, LANES), jnp.float32),
            pltpu.VMEM((nx // LANES, modes * fy_count, LANES), jnp.float32),
        ],
        compiler_params=params(limit),
        name="solve",
    )(total, mode_weights.reshape(1, modes), rows)
    return new_basis.reshape(basis.shape), coefficients


def solution(mesh):
    placed = (
        P("group", None, "space", None),
        P("group", None, "space", None),
        P("group"),
        P("space", None),
        P(),
        P(),
    )
    return jax.shard_map(
        functools.partial(local, mesh.shape["space"]),
        mesh=mesh,
        in_specs=placed,
        out_specs=(P("group", None, "space", None), P("group", None)),
        check_vma=False,
    )
```
